256 devices in a mesh: rep: 4 (over z_lo, core), fsdp: 64 (over y, z_hi, x).
Axes of the slice: x: 4, y: 4, z: 8 (z_hi: 4, z_lo: 2; z = z_hi * 2 + z_lo), core: 2. Of those that a mesh axis runs over, the one named last changes fastest.
Arguments:
- tokens: bfloat16 [32768, 4096], P(('rep', 'fsdp')), may hold values from -24 to 24
- left_factor: bfloat16 [4096, 256], P('fsdp'), may hold values from -0.09375 to 0.09375
- right_factor: bfloat16 [256, 14336], P(None, 'fsdp'), may hold values from -0.375 to 0.375
- tile_values: bfloat16 [128, 128, 128], P('fsdp'), may hold values from -0.5 to 0.5
- tile_rows: int32 [128], P('fsdp'), may hold values from 0 to 31
- tile_cols: int32 [128], P('fsdp'), may hold values from 0 to 111
- grad_out: bfloat16 [32768, 14336], P(('rep', 'fsdp')), may hold values from -6 to 6
Outputs:
- out_rows: bfloat16 [32768, 14336], P(('rep', 'fsdp'))
- input_grad: bfloat16 [32768, 4096], P(('rep', 'fsdp'))
- left_grad: float32 [4096, 256], P('fsdp')
- right_grad: float32 [256, 14336], P(None, 'fsdp')
- tile_grad: float32 [128, 128, 128], P('fsdp')
The draws below stay inside these ranges and needn't reach their ends.
All inputs are finite; a program needn't handle non-finite values.
Results may differ from the reference program's by a relative error of at most 0.0038.
Values may be sent and summed in bfloat16 or wider, within the bound.
A program may use at most 192 MiB of HBM per device.

```python
import math
import jax
import jax.numpy as jnp
import numpy as np
from jax import lax

D = 4096
FF = 14336
R = 256
TB = 128
TOK_DEV = 128
TILES = 128
TOKENS = 32768
N_REP = 4
N_FSDP = 64


def set_ends(values, key, low, largest):
    spot = [jax.random.randint(jax.random.fold_in(key, axis), (), 0, length) for axis, length in enumerate(values.shape)]
    main_axis = values.shape.index(max(values.shape))
    beside = spot[:main_axis] + [(spot[main_axis] + 1) % values.shape[main_axis]] + spot[main_axis + 1:]
    return values.at[tuple(spot)].set(low).at[tuple(beside)].set(largest)


def strengthened(drawn, key, source, target, parts, factor):
    def block_of(dim):
        return (jnp.arange(drawn.shape[dim]) // (drawn.shape[dim] // parts)).reshape((-1,) + (1,) * (drawn.ndim - 1 - dim))

    one_side = jax.random.permutation(key, parts)[block_of(target)]
    far = (block_of(target) + parts // 2) % parts
    return jnp.where((block_of(source) == one_side) | (block_of(source) == far), factor * drawn, drawn)


def levels(stream_key, extent, pieces, smallest, largest):
    gain, own = 1.0, jax.random.fold_in(stream_key, 6)
    for axis_at, parts in pieces:
        heights = jnp.exp(jax.random.uniform(jax.random.fold_in(own, axis_at), (parts,), jnp.float32, smallest / len(pieces), largest / len(pieces)))
        gain = gain * jnp.repeat(heights, extent[axis_at] // parts).reshape([-1 if axis == axis_at else 1 for axis in range(len(extent))])
    return gain


def rank_table(amount, lean):
    portions = [(1 << 20) // math.isqrt(rank ** lean) + 1 for rank in range(1, amount + 1)]
    deviation = 1 + sum(portions) // (1 << 30)
    return np.cumsum(np.array([max(1, weight // deviation) for weight in portions]))


def skewed_ids(stream_key, dims, number_of, slope):
    table = rank_table(number_of, slope)
    ticket = jax.random.randint(jax.random.fold_in(stream_key, 1), dims, 0, int(table[number_of - 1]))
    grade = jnp.searchsorted(jnp.asarray(table, jnp.int32), ticket, side="right")
    return jax.random.permutation(jax.random.fold_in(stream_key, 2), number_of)[grade].astype(jnp.int32)


def scatter_about(rng, dims, width, limit, shards=(), held_as=jnp.bfloat16):
    result = width * jax.random.normal(rng, dims, jnp.float32)
    if shards:
        result = result * levels(rng, dims, shards, -0.22, 0.18)
    return jnp.clip(result, -limit, limit).astype(held_as)


def noise_with(stream_key, dims, spread, reach, split, heavy, kind=jnp.bfloat16):
    result = spread * jax.random.normal(stream_key, dims, jnp.float32)
    if split:
        result = result * levels(stream_key, dims, split, -0.22, 0.18)
    return jnp.clip(strengthened(result, jax.random.fold_in(stream_key, 3), *heavy), -reach, reach).astype(kind)


def setup_inputs(seed: int = 0) -> dict:
    seeds = jax.random.split(jax.random.key(seed), 8)
    tokens = noise_with(seeds[0], (TOKENS, D), 1.0, 24.0, ((0, 256),), (0, 1, 256, 6.0))
    left_factor = scatter_about(seeds[1], (D, R), D ** -0.5, 0.09375, ((0, 64),))
    right_factor = scatter_about(seeds[2], (R, FF), R ** -0.5, 0.375, ((1, 64),))
    tile_values = scatter_about(seeds[3], (TILES, TB, TB), TB ** -0.5, 0.5, ((0, 64),))
    tile_rows = set_ends(jax.random.randint(seeds[4], (TILES,), 0, D // TB), jax.random.fold_in(seeds[4], 1), 0, (D // TB) - 1).astype(jnp.int32)
    tile_cols = set_ends(skewed_ids(seeds[5], (TILES,), FF // TB, 2), jax.random.fold_in(seeds[5], 3), 0, (FF // TB) - 1).astype(jnp.int32)
    grad_out = scatter_about(seeds[6], (TOKENS, FF), 1.0, 6.0, ((0, 256),))
    return dict(tokens=tokens, left_factor=left_factor, right_factor=right_factor, tile_values=tile_values, tile_rows=tile_rows, tile_cols=tile_cols, grad_out=grad_out)


def reference(tokens, left_factor, right_factor, tile_values, tile_rows, tile_cols, grad_out):
    grad_scale = 1.0 / math.sqrt(TOKENS)
    block_rows = TOK_DEV * N_FSDP
    row_blocks = D // TB
    col_blocks = FF // TB
    tiles_wide = tile_values.astype(jnp.float32)
    token_blocks = tokens.reshape(N_REP, block_rows, D)
    grad_blocks = grad_out.reshape(N_REP, block_rows, FF)

    def advance(sums_carry, inputs):
        left_sum, right_sum, tile_sum = sums_carry
        block_tokens, block_grads = inputs
        latent = jnp.dot(block_tokens, left_factor, preferred_element_type=jnp.float32).astype(jnp.bfloat16)
        token_tiles = jnp.take(block_tokens.reshape(block_rows, row_blocks, TB), tile_rows, axis=1).astype(jnp.float32)
        tile_prod = jnp.einsum('tkc,kcd->tkd', token_tiles, tiles_wide)
        sparse_out = jnp.zeros((block_rows, col_blocks, TB), jnp.float32).at[:, tile_cols].add(tile_prod).reshape(block_rows, FF)
        out_rows = (jnp.dot(latent, right_factor, preferred_element_type=jnp.float32) + sparse_out).astype(jnp.bfloat16)
        latent_grad = jnp.dot(block_grads, right_factor.T, preferred_element_type=jnp.float32).astype(jnp.bfloat16)
        grad_tiles = jnp.take(block_grads.reshape(block_rows, col_blocks, TB), tile_cols, axis=1).astype(jnp.float32)
        tile_back = jnp.einsum('tkd,kcd->tkc', grad_tiles, tiles_wide)
        sparse_back = jnp.zeros((block_rows, row_blocks, TB), jnp.float32).at[:, tile_rows].add(tile_back).reshape(block_rows, D)
        input_grad = (jnp.dot(latent_grad, left_factor.T, preferred_element_type=jnp.float32) + sparse_back).astype(jnp.bfloat16)
        left_sum = left_sum + jnp.dot(block_tokens.T, latent_grad, preferred_element_type=jnp.float32) * grad_scale
        right_sum = right_sum + jnp.dot(latent.T, block_grads, preferred_element_type=jnp.float32) * grad_scale
        tile_sum = tile_sum + jnp.einsum('tkc,tkd->kcd', token_tiles, grad_tiles) * grad_scale
        return ((left_sum, right_sum, tile_sum), (out_rows, input_grad))
    start_sums = (jnp.zeros((D, R), jnp.float32), jnp.zeros((R, FF), jnp.float32), jnp.zeros((TILES, TB, TB), jnp.float32))
    final_sums, outputs = lax.scan(advance, start_sums, (token_blocks, grad_blocks))
    out_rows = outputs[0].reshape(TOKENS, FF)
    input_grad = outputs[1].reshape(TOKENS, D)
    return (out_rows, input_grad, final_sums[0], final_sums[1], final_sums[2])
```

```python
import math

import jax
import jax.numpy as jnp
from jax import lax
from jax.experimental import pallas as pl
from jax.experimental.pallas import tpu as pltpu
from jax.sharding import PartitionSpec as P

D = 4096
FF = 14336
TB = 128
R = 256
SIDE = 4
LEFT = 64
RIGHT = 224
GROWS = LEFT + RIGHT + TB + 16
QROWS = LEFT + RIGHT + TB
MESH = pl.DeviceIdType.MESH
BF = jnp.bfloat16
F32 = jnp.float32
Y, H, X = 0, 1, 2
ANY = pl.BlockSpec(memory_space=pl.ANY)
VMEM = pl.BlockSpec(memory_space=pltpu.VMEM)


class Place:
    def __init__(self):
        rep, f = lax.axis_index("rep"), lax.axis_index("fsdp")
        self.l, self.c = rep // 2, rep % 2
        self.at = [f // 16, (f // 4) % 4, f % 4]
        self.s = 2 * self.l - 1
        self.sib = self.dev(core=1 - self.c)
        self.pair = self.dev(low=1 - self.l)
        self.out = self.dev(low=1 - self.l, step=(H, self.s))
        self.plus = {a: self.dev(step=(a, 1)) for a in (Y, X)}
        self.minus = {a: self.dev(step=(a, 3)) for a in (Y, X)}

    def dev(self, core=None, low=None, step=None):
        core = self.c if core is None else core
        low = self.l if low is None else low
        at = list(self.at)
        if step:
            at[step[0]] = (at[step[0]] + step[1] + 4) % 4
        return {"rep": low * 2 + core, "fsdp": (at[0] * 4 + at[1]) * 4 + at[2]}

    def greet(self):
        barrier = pltpu.get_barrier_semaphore()
        near = [self.sib, self.pair, self.out] + [d[a] for d in (self.plus, self.minus) for a in (Y, X)]
        for device in near:
            pl.semaphore_signal(barrier, inc=1, device_id=device, device_id_type=MESH)
        pl.semaphore_wait(barrier, len(near))


class Wire:
    def __init__(self, send_sems, recv_sems):
        self.send_sems, self.recv_sems = send_sems, recv_sems
        self.started = []

    def __call__(self, src, dst, device):
        k = len(self.started)
        copy = pltpu.make_async_remote_copy(
            src_ref=src,
            dst_ref=dst,
            send_sem=self.send_sems.at[k],
            recv_sem=self.recv_sems.at[k],
            device_id=device,
            device_id_type=MESH,
        )
        copy.start()
        self.started.append(copy)
        return copy

    def finish(self):
        for copy in self.started:
            copy.wait_send()


def interleave(parts):
    parts = list(parts)
    while parts:
        for part in list(parts):
            try:
                next(part)
            except StopIteration:
                parts.remove(part)


def view(ref, fixed, axis, j, row0, rows, half=None, chunk=None, chunks=1):
    sel = list(fixed)
    sel[axis] = j
    r0, n = row0, rows
    free = [a for a in range(3) if a != axis and fixed[a] is None]
    if half is not None:
        if free:
            width = 2 // chunks
            start = half * 2 + (0 if chunk is None else chunk * width)
            sel[free[0]] = pl.ds(start, width if chunk is not None else 2)
        elif rows % 32 == 0:
            n = rows // 2
            r0 = row0 + half * n
        else:
            cut = (rows // 32 + 1) * 16
            r0, n = (row0, cut) if half == 0 else (row0 + cut, rows - cut)
    sel = [slice(None) if v is None else v for v in sel]
    return ref.at[sel[0], sel[1], sel[2], pl.ds(r0, n), :]


GATHER = (((X, Y, H), 0, 144), ((Y, H, X), 144, 160), ((H, X, Y), 304, 128))


def gather_kernel(pay, tok, grad, full, tok_s, grad_s, send_sems, recv_sems, local_sem, side_sems, wide_sems):
    me = Place()
    mine = full.at[me.c]
    own = pltpu.make_async_copy(pay.at[me.c], mine.at[me.at[0], me.at[1], me.at[2]], local_sem)
    own.start()
    me.greet()
    wire = Wire(send_sems, recv_sems)

    def to_sibling(src, dst, pair):
        return pltpu.make_async_remote_copy(
            src_ref=src,
            dst_ref=dst,
            send_sem=pair.at[0],
            recv_sem=pair.at[1],
            device_id=me.sib,
            device_id_type=MESH,
        )

    def part(order, row0, rows):
        for stage, axis in enumerate(order):
            fixed = [None if a in order[:stage] else me.at[a] for a in range(3)]
            last = stage == 2

            def blk(j, half=None, chunk=None, chunks=1):
                return view(mine, fixed, axis, j, row0, rows, half, chunk, chunks)

            def src(j, half, chunk=None, chunks=1):
                if stage:
                    return blk(j, half, chunk, chunks)
                return view(pay.at[pl.ds(me.c, 1)].reshape(1, 1, 1, GROWS, TB), [0, 0, 0], axis, 0, row0, rows, half)

            def got(ref):
                if last:
                    to_sibling(ref, ref, side_sems).start()

            def send(j, half, device, chunk=None, chunks=1, first=False):
                ref = blk(j, half, chunk, chunks)
                return wire(ref, ref, device)

            i = me.at[axis]
            if last:
                got(blk(i))
            if axis == H:
                l, s = me.l, me.s
                up, down, across = (i + s + 4) % 4, (i - s + 4) % 4, (i + 2) % 4
                chunks = 2 if last else 1
                ids = range(chunks) if last else (None,)
                a = [send(i, 1 - l, me.out, q, chunks) for q in ids]
                b = [send(i, l, me.out, q, chunks) for q in ids]
                yield
                f = []
                for k, q in enumerate(ids):
                    a[k].wait_recv()
                    f.append(send(up, l, me.pair, q, chunks))
                    got(blk(up, l, q, chunks))
                yield
                e = []
                for k, q in enumerate(ids):
                    b[k].wait_recv()
                    e.append(send(up, 1 - l, me.pair, q, chunks))
                    got(blk(up, 1 - l, q, chunks))
                yield
                g = []
                for k, q in enumerate(ids):
                    f[k].wait_recv()
                    g.append(send(down, 1 - l, me.out, q, chunks))
                    got(blk(down, 1 - l, q, chunks))
                yield
                for k, q in enumerate(ids):
                    e[k].wait_recv()
                    got(blk(down, l, q, chunks))
                w = []
                for k, q in enumerate(ids):
                    g[k].wait_recv()
                    w.append(send(across, l, me.pair, q, chunks))
                    got(blk(across, l, q, chunks))
                yield
                for k, q in enumerate(ids):
                    w[k].wait_recv()
                    got(blk(across, 1 - l, q, chunks))
            else:
                plus, minus = me.plus[axis], me.minus[axis]
                after, before, across = (i + 1) % 4, (i + 3) % 4, (i + 2) % 4
                a0, b1 = send(i, 0, plus), send(i, 1, minus)
                a1, b0 = send(i, 1, plus), send(i, 0, minus)
                yield
                a0.wait_recv()
                c0 = send(before, 0, plus)
                got(blk(before, 0))
                b1.wait_recv()
                c1 = send(after, 1, minus)
                got(blk(after, 1))
                yield
                a1.wait_recv()
                got(blk(before, 1))
                b0.wait_recv()
                got(blk(after, 0))
                yield
                c0.wait_recv()
                got(blk(across, 0))
                c1.wait_recv()
                got(blk(across, 1))

    own.wait()
    runs = [part(*p) for p in GATHER]
    for run in runs:
        next(run)
    swaps = [to_sibling(tok, tok_s, wide_sems.at[0]), to_sibling(grad, grad_s, wide_sems.at[1])]
    for swap in swaps:
        swap.start()
    interleave(runs)
    wire.finish()
    for swap in swaps:
        swap.wait()
    whole = to_sibling(mine, full.at[1 - me.c], side_sems)
    whole.wait()


def gather(pay, tok, grad):
    return pl.pallas_call(
        gather_kernel,
        out_shape=(
            jax.ShapeDtypeStruct((2, SIDE, SIDE, SIDE, GROWS, TB), BF),
            jax.ShapeDtypeStruct(tok.shape, BF),
            jax.ShapeDtypeStruct(grad.shape, BF),
        ),
        in_specs=[ANY] * 3,
        out_specs=(ANY,) * 3,
        scratch_shapes=[
            pltpu.SemaphoreType.DMA((80,)),
            pltpu.SemaphoreType.DMA((80,)),
            pltpu.SemaphoreType.DMA,
            pltpu.SemaphoreType.DMA((2,)),
            pltpu.SemaphoreType.DMA((2, 2)),
        ],
        compiler_params=pltpu.CompilerParams(collective_id=0, has_side_effects=True),
        name="gather_factors",
    )(pay, tok, grad)


REDUCE = (((H, Y, X), 0, 144), ((X, H, Y), 144, 144), ((Y, X, H), 288, 128))


def add_into(dst, *terms):
    shape = dst.shape
    lead = shape[:-2]
    rows = shape[-2]
    count = math.prod(lead)

    def body(k, _):
        at = []
        for n in reversed(lead):
            at.append(k % n)
            k = k // n
        at = tuple(reversed(at))
        for r in range(0, rows, 16):
            here = at + (pl.ds(r, 16), slice(None))
            total = terms[0][here].astype(F32)
            for term in terms[1:]:
                total = total + term[here].astype(F32)
            dst[here] = total.astype(dst.dtype)
        return 0

    if count == 1:
        body(0, 0)
    else:
        lax.fori_loop(0, count, body, 0)


def reduce_kernel(scale, q_ref, out, *scratch):
    (send_sems, recv_sems), scratch = scratch[:2], scratch[2:]
    me = Place()
    me.greet()
    wire = Wire(send_sems, recv_sems)
    per_part = len(scratch) // 3

    def part(n):
        order, row0, rows = REDUCE[n]
        pool = list(scratch[n * per_part : (n + 1) * per_part])
        held = q_ref
        for stage, axis in enumerate(order):
            fixed = [me.at[a] if a in order[:stage] else None for a in range(3)]
            if stage:
                fixed = [0 if a in order[:stage] else None for a in range(3)]
            base = row0 if stage == 0 else 0
            staged = held if stage != 1 else pool.pop(0)
            nxt = pool.pop(0)
            first, second, third = pool.pop(0), pool.pop(0), pool.pop(0)
            dims = [a for a in range(3) if a != axis and fixed[a] is None]
            i = me.at[axis]

            def blk(ref, j, half=None, chunk=None, chunks=1):
                at0 = base if ref is held or ref is staged else 0
                return view(ref, fixed, axis, j, at0, rows, half, chunk, chunks)

            def send(j, half, dst, dst_j, device, extra=None, chunk=None, chunks=1):
                src = blk(staged, j, half, chunk, chunks)
                if extra is not None:
                    add_into(src, blk(held, j, half, chunk, chunks), extra)
                elif staged is not held:
                    add_into(src, blk(held, j, half, chunk, chunks))
                return wire(src, blk(dst, dst_j, half, chunk, chunks), device)

            if axis == H:
                l, s = me.l, me.s
                up, down, across = (i + s + 4) % 4, (i - s + 4) % 4, (i + 2) % 4
                chunks = 2 if stage == 0 else 1
                ids = range(chunks) if stage == 0 else (None,)
                a = [send(across, l, first, 0, me.pair, None, q, chunks) for q in ids]
                b = [send(down, 1 - l, second, 0, me.pair, None, q, chunks) for q in ids]
                yield
                c = []
                for k, q in enumerate(ids):
                    a[k].wait_recv()
                    c.append(send(across, 1 - l, first, 1, me.out, blk(first, 0, 1 - l, q, chunks), q, chunks))
                yield
                d = []
                for k, q in enumerate(ids):
                    b[k].wait_recv()
                    d.append(send(up, l, third, 0, me.out, blk(second, 0, l, q, chunks), q, chunks))
                yield
                e = []
                for k, q in enumerate(ids):
                    c[k].wait_recv()
                    e.append(send(down, l, second, 0, me.pair, blk(first, 1, l, q, chunks), q, chunks))
                yield
                f = []
                for k, q in enumerate(ids):
                    e[k].wait_recv()
                    f.append(send(up, 1 - l, third, 0, me.out, blk(second, 0, 1 - l, q, chunks), q, chunks))
                yield
                for k, q in enumerate(ids):
                    d[k].wait_recv()
                    add_into(blk(nxt, 0, 1 - l, q, chunks), blk(held, i, 1 - l, q, chunks), blk(third, 0, 1 - l, q, chunks))
                yield
                for k, q in enumerate(ids):
                    f[k].wait_recv()
                    add_into(blk(nxt, 0, l, q, chunks), blk(held, i, l, q, chunks), blk(third, 0, l, q, chunks))
            else:
                plus, minus = me.plus[axis], me.minus[axis]
                after, before, across = (i + 1) % 4, (i + 3) % 4, (i + 2) % 4
                a0 = send(across, 0, first, 0, plus)
                a1 = send(across, 1, first, 0, minus)
                b1 = send(after, 1, second, 0, plus)
                b0 = send(before, 0, third, 0, minus)
                yield
                a0.wait_recv()
                c0 = send(after, 0, second, 0, plus, blk(first, 0, 0))
                a1.wait_recv()
                c1 = send(before, 1, third, 0, minus, blk(first, 0, 1))
                yield
                b1.wait_recv()
                b0.wait_recv()
                yield
                c0.wait_recv()
                c1.wait_recv()
                for half in (0, 1):
                    add_into(blk(nxt, 0, half), blk(held, i, half), blk(second, 0, half), blk(third, 0, half))
            held = nxt
            yield
        other = pool.pop(0)
        swap = wire(held, other, me.pair)
        yield
        swap.wait_recv()
        place = out.at[me.c, pl.ds(row0, rows), :]
        place[...] = (held[0, 0, 0] + other[0, 0, 0]) * scale
        final = wire(place, place, me.sib)
        yield
        final.wait_recv()

    interleave([part(n) for n in range(3)])
    wire.finish()


def reduce_scratch():
    shapes = []
    for order, _, rows in REDUCE:
        dims = [SIDE] * 3
        for stage, axis in enumerate(order):
            if stage == 1:
                shapes.append(pltpu.VMEM(tuple(dims) + (rows, TB), BF))
            wire = BF if stage < 2 else F32
            dims[axis] = 1
            shapes.append(pltpu.VMEM(tuple(dims) + (rows, TB), F32))
            two = list(dims)
            two[axis] = 2
            shapes.append(pltpu.VMEM(tuple(two if axis == H else dims) + (rows, TB), wire))
            shapes += [pltpu.VMEM(tuple(dims) + (rows, TB), wire)] * 2
        shapes.append(pltpu.VMEM((1, 1, 1, rows, TB), F32))
    return shapes


def reduce(q, scale):
    return pl.pallas_call(
        lambda *refs: reduce_kernel(scale, *refs),
        out_shape=jax.ShapeDtypeStruct((2, QROWS, TB), F32),
        in_specs=[VMEM],
        out_specs=VMEM,
        scratch_shapes=[pltpu.SemaphoreType.DMA((80,)), pltpu.SemaphoreType.DMA((80,))] + reduce_scratch(),
        compiler_params=pltpu.CompilerParams(
            collective_id=1, has_side_effects=True, vmem_limit_bytes=40 * 1024 * 1024
        ),
        name="reduce_gradients",
    )(q)


def contract_rows(left, right):
    return lax.dot_general(left, right, (((0,), (0,)), ((), ())), preferred_element_type=F32)


def contract_cols(left, right):
    return lax.dot_general(left, right, (((1,), (1,)), ((), ())), preferred_element_type=F32)


def local(tokens, left_factor, right_factor, tile_values, tile_rows, tile_cols, grad_out):
    here = tokens.shape[0]
    grad_scale = 1.0 / math.sqrt(here * lax.axis_size("fsdp") * lax.axis_size("rep"))
    core = lax.axis_index("rep") % 2
    row_blocks, col_blocks = D // TB, FF // TB
    places = jnp.stack([tile_rows, tile_cols], 1).astype(BF)
    pay = jnp.concatenate(
        [
            left_factor.reshape(LEFT, 2, TB).transpose(1, 0, 2),
            right_factor.T.reshape(RIGHT, 2, TB).transpose(1, 0, 2),
            tile_values,
            jnp.broadcast_to(jnp.pad(places, ((0, 0), (0, TB - 2)))[:, None, :], (2, 16, TB)),
        ],
        1,
    )
    full, tok_s, grad_s = gather(pay, tokens, grad_out)
    full = full.reshape(2, 64, GROWS, TB)
    left_all = full[:, :, :LEFT].reshape(2, D, TB).transpose(1, 0, 2).reshape(D, R)
    right_all = full[:, :, LEFT : LEFT + RIGHT].reshape(2, FF, TB).transpose(1, 0, 2).reshape(FF, R)
    tiles_all = full[:, :, LEFT + RIGHT : QROWS].transpose(1, 0, 2, 3).reshape(128, TB, TB)
    index = full[:, :, QROWS, :2].astype(jnp.int32)
    rows_all = index[:, :, 0].T.reshape(128)
    cols_all = index[:, :, 1].T.reshape(128)

    both_tok = jnp.concatenate([tokens, tok_s], 0)
    both_grad = jnp.concatenate([grad_out, grad_s], 0)
    latent2 = jnp.dot(both_tok, left_all, preferred_element_type=F32).astype(BF)
    back2 = jnp.dot(both_grad, right_all, preferred_element_type=F32).astype(BF)
    latent, latent_grad = latent2[:here], back2[:here]

    token_tiles = jnp.take(tokens.reshape(here, row_blocks, TB), rows_all, axis=1)
    tile_prod = jnp.einsum("tkc,kcd->tkd", token_tiles, tiles_all, preferred_element_type=F32)
    sparse_out = jnp.zeros((here, col_blocks, TB), F32).at[:, cols_all].add(tile_prod).reshape(here, FF)
    out_rows = (contract_cols(latent, right_all) + sparse_out).astype(BF)
    grad_tiles = jnp.take(grad_out.reshape(here, col_blocks, TB), cols_all, axis=1)
    tile_back = jnp.einsum("tkd,kcd->tkc", grad_tiles, tiles_all, preferred_element_type=F32)
    sparse_back = jnp.zeros((here, row_blocks, TB), F32).at[:, rows_all].add(tile_back).reshape(here, D)
    input_grad = (contract_cols(latent_grad, left_all) + sparse_back).astype(BF)

    lat_h = lax.dynamic_slice_in_dim(latent2, core * TB, TB, 1)
    back_h = lax.dynamic_slice_in_dim(back2, core * TB, TB, 1)
    rows_h = lax.dynamic_index_in_dim(index[:, :, 0], core, 0, False)
    cols_h = lax.dynamic_index_in_dim(index[:, :, 1], core, 0, False)
    tok_h = jnp.take(both_tok.reshape(2 * here, row_blocks, TB), rows_h, axis=1)
    grad_h = jnp.take(both_grad.reshape(2 * here, col_blocks, TB), cols_h, axis=1)
    q = jnp.concatenate(
        [
            contract_rows(both_tok, back_h).astype(BF).reshape(64, LEFT, TB),
            contract_rows(both_grad, lat_h).astype(BF).reshape(64, RIGHT, TB),
            jnp.einsum("tkc,tkd->kcd", tok_h, grad_h, preferred_element_type=F32).astype(BF),
        ],
        1,
    ).reshape(SIDE, SIDE, SIDE, QROWS, TB)
    total = reduce(q, grad_scale)
    left_grad = total[:, :LEFT].transpose(1, 0, 2).reshape(LEFT, R)
    right_grad = total[:, LEFT : LEFT + RIGHT].transpose(0, 2, 1).reshape(R, RIGHT)
    return (out_rows, input_grad, left_grad, right_grad, total[:, LEFT + RIGHT :])


def solution(mesh):
    placed = (
        P(("rep", "fsdp"), None),
        P("fsdp", None),
        P(None, "fsdp"),
        P("fsdp", None, None),
        P("fsdp"),
        P("fsdp"),
        P(("rep", "fsdp"), None),
    )
    return jax.shard_map(
        local,
        mesh=mesh,
        in_specs=placed,
        out_specs=(
            P(("rep", "fsdp"), None),
            P(("rep", "fsdp"), None),
            P("fsdp", None),
            P(None, "fsdp"),
            P("fsdp", None, None),
        ),
        check_vma=False,
    )
```

```python
import math

import jax
import jax.numpy as jnp
from jax import lax
from jax.experimental import pallas as pl
from jax.experimental.pallas import tpu as pltpu
from jax.sharding import PartitionSpec as P

D = 4096
FF = 14336
TB = 128
R = 256
SIDE = 4
LEFT = 64
RIGHT = 224
GROWS = LEFT + RIGHT + TB + 16
QROWS = LEFT + RIGHT + TB
MESH = pl.DeviceIdType.MESH
BF = jnp.bfloat16
F32 = jnp.float32
Y, H, X = 0, 1, 2
ANY = pl.BlockSpec(memory_space=pl.ANY)
VMEM = pl.BlockSpec(memory_space=pltpu.VMEM)


class Place:
    def __init__(self):
        rep, f = lax.axis_index("rep"), lax.axis_index("fsdp")
        self.l, self.c = rep // 2, rep % 2
        self.at = [f // 16, (f // 4) % 4, f % 4]
        self.s = 2 * self.l - 1
        self.sib = self.dev(core=1 - self.c)
        self.pair = self.dev(low=1 - self.l)
        self.out = self.dev(low=1 - self.l, step=(H, self.s))
        self.plus = {a: self.dev(step=(a, 1)) for a in (Y, X)}
        self.minus = {a: self.dev(step=(a, 3)) for a in (Y, X)}
        self.direct = {a: [self.dev(step=(a, k)) for k in (1, 3, 2)] for a in (Y, X)}
        self.direct[H] = [self.out, self.dev(step=(H, self.s)), self.dev(low=1 - self.l, step=(H, 2))]
        self.behind = self.dev(step=(H, -self.s))

    def dev(self, core=None, low=None, step=None):
        core = self.c if core is None else core
        low = self.l if low is None else low
        at = list(self.at)
        if step:
            at[step[0]] = (at[step[0]] + step[1] + 4) % 4
        return {"rep": low * 2 + core, "fsdp": (at[0] * 4 + at[1]) * 4 + at[2]}

    def greet(self):
        barrier = pltpu.get_barrier_semaphore()
        near = [self.sib, self.pair, self.behind] + [d for a in (Y, H, X) for d in self.direct[a]]
        for device in near:
            pl.semaphore_signal(barrier, inc=1, device_id=device, device_id_type=MESH)
        pl.semaphore_wait(barrier, len(near))


class Wire:
    def __init__(self, send_sems, recv_sems):
        self.send_sems, self.recv_sems = send_sems, recv_sems
        self.started = []

    def __call__(self, src, dst, device):
        k = len(self.started)
        copy = pltpu.make_async_remote_copy(
            src_ref=src,
            dst_ref=dst,
            send_sem=self.send_sems.at[k],
            recv_sem=self.recv_sems.at[k],
            device_id=device,
            device_id_type=MESH,
        )
        copy.start()
        self.started.append(copy)
        return copy

    def finish(self):
        for copy in self.started:
            copy.wait_send()


def view(ref, fixed, axis, j, row0, rows, half=None, chunk=None, chunks=1):
    sel = list(fixed)
    sel[axis] = j
    r0, n = row0, rows
    free = [a for a in range(3) if a != axis and fixed[a] is None]
    if half is not None:
        if free:
            width = 2 // chunks
            start = half * 2 + (0 if chunk is None else chunk * width)
            sel[free[0]] = pl.ds(start, width if chunk is not None else 2)
        elif rows % 32 == 0:
            n = rows // 2
            r0 = row0 + half * n
        else:
            cut = (rows // 32 + 1) * 16
            r0, n = (row0, cut) if half == 0 else (row0 + cut, rows - cut)
    sel = [slice(None) if v is None else v for v in sel]
    return ref.at[sel[0], sel[1], sel[2], pl.ds(r0, n), :]


GATHER = (((X, Y, H), 0, 80), ((Y, H, X), 80, 176), ((H, X, Y), 256, 176))


def run_all(active):
    while active:
        for run in list(active):
            try:
                next(run)
            except StopIteration:
                active.remove(run)


def spread(me, axis, send, got, ready):
    i = me.at[axis]
    across = (i + 2) % 4
    if axis == H:
        l, s = me.l, me.s
        up, down = (i + s + 4) % 4, (i - s + 4) % 4
        a, b = send(i, 1 - l, me.out), send(i, l, me.out)
        yield
        a.wait_recv()
        f = send(up, l, me.pair)
        got(up, l)
        yield
        b.wait_recv()
        e = send(up, 1 - l, me.pair)
        got(up, 1 - l)
        ready(up)
        yield
        f.wait_recv()
        g = send(down, 1 - l, me.out)
        got(down, 1 - l)
        yield
        e.wait_recv()
        got(down, l)
        ready(down)
        yield
        g.wait_recv()
        w = send(across, l, me.pair)
        got(across, l)
        yield
        w.wait_recv()
        got(across, 1 - l)
        ready(across)
    else:
        plus, minus = me.plus[axis], me.minus[axis]
        after, before = (i + 1) % 4, (i + 3) % 4
        a0, b1 = send(i, 0, plus), send(i, 1, minus)
        a1, b0 = send(i, 1, plus), send(i, 0, minus)
        yield
        a0.wait_recv()
        c0 = send(before, 0, plus)
        got(before, 0)
        b1.wait_recv()
        c1 = send(after, 1, minus)
        got(after, 1)
        yield
        a1.wait_recv()
        got(before, 1)
        ready(before)
        b0.wait_recv()
        got(after, 0)
        ready(after)
        yield
        c0.wait_recv()
        got(across, 0)
        c1.wait_recv()
        got(across, 1)
        ready(across)


def gather_kernel(pay, tok, grad, full, tok_s, grad_s, send_sems, recv_sems, local_sem, side_sems, wide_sems):
    me = Place()
    mine = full.at[me.c]
    own = pltpu.make_async_copy(pay.at[me.c], mine.at[me.at[0], me.at[1], me.at[2]], local_sem)
    own.start()
    me.greet()
    own.wait()
    wire = Wire(send_sems, recv_sems)
    active = []

    def to_sibling(src, dst, pair):
        return pltpu.make_async_remote_copy(
            src_ref=src,
            dst_ref=dst,
            send_sem=pair.at[0],
            recv_sem=pair.at[1],
            device_id=me.sib,
            device_id_type=MESH,
        )

    def part(order, row0, rows):
        one, two, three = order

        def piece(at, half=None):
            sel = [at.get(a, slice(None)) for a in range(3)]
            if half is not None:
                sel[one] = pl.ds(half * 2, 2)
            return mine.at[sel[0], sel[1], sel[2], pl.ds(row0, rows), :]

        def last(j2):
            def send(j, half, device):
                ref = piece({two: j2, three: j}, half)
                return wire(ref, ref, device)

            def got(j, half):
                ref = piece({two: j2, three: j}, half)
                to_sibling(ref, ref, side_sems).start()

            ref = piece({two: j2, three: me.at[three]})
            to_sibling(ref, ref, side_sems).start()
            return spread(me, three, send, got, lambda j: None)

        def start_last(j2):
            run = last(j2)
            next(run)
            active.append(run)

        def send(j, half, device):
            ref = piece({two: j, three: me.at[three]}, half)
            return wire(ref, ref, device)

        seed = piece({a: me.at[a] for a in range(3)})
        seeds = [wire(seed, seed, device) for device in me.direct[one]]
        yield
        for copy in seeds:
            copy.wait_recv()
        run = spread(me, two, send, lambda j, half: None, start_last)
        next(run)
        start_last(me.at[two])
        active.append(run)

    for p in GATHER:
        active.append(part(*p))
    for run in active:
        next(run)
    swaps = [to_sibling(tok, tok_s, wide_sems.at[0]), to_sibling(grad, grad_s, wide_sems.at[1])]
    for swap in swaps:
        swap.start()
    run_all(active)
    wire.finish()
    for swap in swaps:
        swap.wait()
    whole = to_sibling(mine, full.at[1 - me.c], side_sems)
    whole.wait()


def gather(pay, tok, grad):
    return pl.pallas_call(
        gather_kernel,
        out_shape=(
            jax.ShapeDtypeStruct((2, SIDE, SIDE, SIDE, GROWS, TB), BF),
            jax.ShapeDtypeStruct(tok.shape, BF),
            jax.ShapeDtypeStruct(grad.shape, BF),
        ),
        in_specs=[ANY] * 3,
        out_specs=(ANY,) * 3,
        scratch_shapes=[
            pltpu.SemaphoreType.DMA((120,)),
            pltpu.SemaphoreType.DMA((120,)),
            pltpu.SemaphoreType.DMA,
            pltpu.SemaphoreType.DMA((2,)),
            pltpu.SemaphoreType.DMA((2, 2)),
        ],
        compiler_params=pltpu.CompilerParams(collective_id=0, has_side_effects=True),
        name="gather_factors",
    )(pay, tok, grad)


REDUCE = (((H, Y, X), 0, 144), ((X, H, Y), 144, 144), ((Y, X, H), 288, 128))


def add_into(dst, *terms):
    shape = dst.shape
    lead = shape[:-2]
    rows = shape[-2]
    count = math.prod(lead)

    def body(k, _):
        at = []
        for n in reversed(lead):
            at.append(k % n)
            k = k // n
        at = tuple(reversed(at))
        for r in range(0, rows, 16):
            here = at + (pl.ds(r, 16), slice(None))
            total = terms[0][here].astype(F32)
            for term in terms[1:]:
                total = total + term[here].astype(F32)
            dst[here] = total.astype(dst.dtype)
        return 0

    if count == 1:
        body(0, 0)
    else:
        lax.fori_loop(0, count, body, 0)


def reduce_parts(me, scale, q_ref, out, scratch):
    (send_sems, recv_sems), scratch = scratch[:2], scratch[2:]
    wire = Wire(send_sems, recv_sems)
    per_part = len(scratch) // 3

    def part(n):
        order, row0, rows = REDUCE[n]
        pool = list(scratch[n * per_part : (n + 1) * per_part])
        held = q_ref
        for stage, axis in enumerate(order):
            fixed = [me.at[a] if a in order[:stage] else None for a in range(3)]
            if stage:
                fixed = [0 if a in order[:stage] else None for a in range(3)]
            base = row0 if stage == 0 else 0
            staged = held
            nxt = pool.pop(0)
            first, second, third = pool.pop(0), pool.pop(0), pool.pop(0)
            dims = [a for a in range(3) if a != axis and fixed[a] is None]
            i = me.at[axis]

            def blk(ref, j, half=None, chunk=None, chunks=1):
                at0 = base if ref is held or ref is staged else 0
                return view(ref, fixed, axis, j, at0, rows, half, chunk, chunks)

            def send(j, half, dst, dst_j, device, extra=None, chunk=None, chunks=1):
                src = blk(staged, j, half, chunk, chunks)
                if extra is not None:
                    add_into(src, blk(held, j, half, chunk, chunks), extra)
                return wire(src, blk(dst, dst_j, half, chunk, chunks), device)

            if axis == H:
                l, s = me.l, me.s
                up, down, across = (i + s + 4) % 4, (i - s + 4) % 4, (i + 2) % 4
                chunks = 2 if stage == 0 else 1
                ids = range(chunks) if stage == 0 else (None,)
                a = [send(across, l, first, 0, me.pair, None, q, chunks) for q in ids]
                b = [send(down, 1 - l, second, 0, me.pair, None, q, chunks) for q in ids]
                yield
                c = []
                for k, q in enumerate(ids):
                    a[k].wait_recv()
                    c.append(send(across, 1 - l, first, 1, me.out, blk(first, 0, 1 - l, q, chunks), q, chunks))
                yield
                d = []
                for k, q in enumerate(ids):
                    b[k].wait_recv()
                    d.append(send(up, l, third, 0, me.out, blk(second, 0, l, q, chunks), q, chunks))
                yield
                e = []
                for k, q in enumerate(ids):
                    c[k].wait_recv()
                    e.append(send(down, l, second, 0, me.pair, blk(first, 1, l, q, chunks), q, chunks))
                yield
                f = []
                for k, q in enumerate(ids):
                    e[k].wait_recv()
                    f.append(send(up, 1 - l, third, 0, me.out, blk(second, 0, 1 - l, q, chunks), q, chunks))
                yield
                for k, q in enumerate(ids):
                    d[k].wait_recv()
                    add_into(blk(nxt, 0, 1 - l, q, chunks), blk(held, i, 1 - l, q, chunks), blk(third, 0, 1 - l, q, chunks))
                yield
                for k, q in enumerate(ids):
                    f[k].wait_recv()
                    add_into(blk(nxt, 0, l, q, chunks), blk(held, i, l, q, chunks), blk(third, 0, l, q, chunks))
            else:
                plus, minus = me.plus[axis], me.minus[axis]
                after, before, across = (i + 1) % 4, (i + 3) % 4, (i + 2) % 4
                a0 = send(across, 0, first, 0, plus)
                a1 = send(across, 1, first, 0, minus)
                b1 = send(after, 1, second, 0, plus)
                b0 = send(before, 0, third, 0, minus)
                yield
                a0.wait_recv()
                c0 = send(after, 0, second, 0, plus, blk(first, 0, 0))
                a1.wait_recv()
                c1 = send(before, 1, third, 0, minus, blk(first, 0, 1))
                yield
                b1.wait_recv()
                b0.wait_recv()
                yield
                c0.wait_recv()
                c1.wait_recv()
                for half in (0, 1):
                    add_into(blk(nxt, 0, half), blk(held, i, half), blk(second, 0, half), blk(third, 0, half))
            held = nxt
            yield
        other = pool.pop(0)
        swap = wire(held, other, me.pair)
        yield
        swap.wait_recv()
        place = out.at[me.c, pl.ds(row0, rows), :]
        place[...] = (held[0, 0, 0] + other[0, 0, 0]) * scale
        final = wire(place, place, me.sib)
        yield
        final.wait_recv()

    return [part(n) for n in range(3)] + [wire.finish]


def reduce_scratch():
    shapes = []
    for order, _, rows in REDUCE:
        dims = [SIDE] * 3
        for stage, axis in enumerate(order):
            wire = BF if stage < 1 else F32
            dims[axis] = 1
            shapes.append(pltpu.VMEM(tuple(dims) + (rows, TB), F32))
            two = list(dims)
            two[axis] = 2
            shapes.append(pltpu.VMEM(tuple(two if axis == H else dims) + (rows, TB), wire))
            shapes += [pltpu.VMEM(tuple(dims) + (rows, TB), wire)] * 2
        shapes.append(pltpu.VMEM((1, 1, 1, rows, TB), F32))
    return shapes


def run_with(active, work):
    while active:
        for run in list(active):
            try:
                next(run)
            except StopIteration:
                active.remove(run)
        next(work, None)
    for _ in work:
        pass


CHUNKS = 8
PER = 64 // CHUNKS
WIDE = PER * RIGHT
SLICES = 4
EMPTY = 128
PIECE = 2048


def contract_rows(left, right):
    return lax.dot_general(left, right, (((0,), (0,)), ((), ())), preferred_element_type=F32)


def contract_cols(left, right):
    return lax.dot_general(left, right, (((1,), (1,)), ((), ())), preferred_element_type=F32)


def dot(left, right):
    return jnp.dot(left, right, preferred_element_type=F32)


def wide(ref, first, count, rows=None):
    return jnp.concatenate([ref[n] if rows is None else ref[n, :rows] for n in range(first, first + count)], 1)


def load(src, dst, sem):
    copy = pltpu.make_async_copy(src, dst, sem)
    copy.start()
    return copy


def products_kernel(scale, places, order, same, full, tok, tok_s, grad, grad_s, total, out, back_out, *scratch):
    (q, left, right, tiles, tok2, grad2, run, latent, latent_o, back_c, back_o, stage) = scratch[:12]
    left_sems, right_sems, tile_sem, stage_sems = scratch[12:16]
    me = Place()
    c, o = me.c, 1 - me.c
    here = tok.shape[0]
    pieces = [(tok, tok_s, tok2, n) for n in range(D // PIECE)] + [(grad, grad_s, grad2, n) for n in range(FF // PIECE)]

    def fetch(k):
        own, other, _, n = pieces[k]
        span = pl.ds(n * PIECE, PIECE)
        return [
            load(own.at[:, span], stage.at[k % 3, pl.ds(0, here)], stage_sems.at[0, k % 3]),
            load(other.at[:, span], stage.at[k % 3, pl.ds(here, here)], stage_sems.at[1, k % 3]),
        ]

    coming = [fetch(k) for k in range(3)]
    left_in, right_in = [], []
    for k, half in enumerate((c, o)):
        left_in.append(load(full.at[half, :, pl.ds(0, LEFT), :], left.at[k], left_sems.at[k]))
        right_in.append(load(full.at[half, :, pl.ds(LEFT, RIGHT), :], right.at[k], right_sems.at[k]))
    tiles_in = load(full.at[:, :, pl.ds(LEFT + RIGHT, TB), :], tiles, tile_sem)
    me.greet()
    runs = reduce_parts(me, scale, q, total, scratch[16:])

    def tile_part(g, _):
        for u in range(8):
            t = 2 * (g * 8 + u) + c
            part = contract_rows(tok2[places[0, t]], grad2[places[1, t]])
            q[g // 2, (g % 2) * 2 + u // 4, u % 4, LEFT + RIGHT :, :] = part.astype(BF)
        return 0

    for k, (_, _, held, n) in enumerate(pieces):
        for copy in coming[k]:
            copy.wait()
        for b in range(PIECE // TB):
            held[n * (PIECE // TB) + b] = stage[k % 3, :, b * TB : (b + 1) * TB]
        if k + 3 < len(pieces):
            coming.append(fetch(k + 3))
    lax.fori_loop(0, 8, tile_part, 0)
    next(runs[2])

    left_in[0].wait()
    latent[...] = dot(wide(tok2, 0, D // TB), left[0].reshape(D, TB)).astype(BF)
    right_in[0].wait()
    back = jnp.zeros((2 * here, TB), F32)
    for j in range(CHUNKS):
        part = wide(grad2, j * WIDE // TB, WIDE // TB)
        back = back + dot(part, right[0, j * PER : (j + 1) * PER].reshape(WIDE, TB))
        q[j // 2, (j % 2) * 2 : (j % 2) * 2 + 2, :, LEFT : LEFT + RIGHT, :] = (
            contract_rows(part, latent[...]).astype(BF).reshape(2, 4, RIGHT, TB)
        )
    next(runs[1])
    back_c[...] = back.astype(BF)
    for j in range(4):
        part = contract_rows(wide(tok2, j * 8, 8), back_c[...])
        q[j, :, :, :LEFT, :] = part.astype(BF).reshape(4, 4, LEFT, TB)
    next(runs[0])

    def running_sums(which, product, g0):
        def body(g, held):
            parts = [product(g * 8 + u) for u in range(8)]
            for u in range(8):
                t = g * 8 + u
                held = held * same[which, t] + parts[u]
                run[t] = held
            return held

        before = jnp.zeros((here, TB), F32) if g0 == 0 else run[g0 * 8 - 1]
        lax.fori_loop(g0, g0 + 16 // SLICES, body, before)

    def ahead(t):
        return dot(tok2[order[0, 0, t], :here], tiles[order[0, 1, t], order[0, 2, t]])

    def behind(t):
        return contract_cols(grad2[order[1, 0, t], :here], tiles[order[1, 1, t], order[1, 2, t]])

    def work():
        left_in[1].wait()
        latent_o[...] = dot(wide(tok2, 0, D // TB, here), left[1].reshape(D, TB)).astype(BF)
        tiles_in.wait()
        run[EMPTY] = jnp.zeros((here, TB), F32)
        for n in range(SLICES):
            running_sums(0, ahead, n * 16 // SLICES)
            yield
        right_in[1].wait()
        back_o[...] = jnp.zeros((here, TB), F32)
        for j in range(CHUNKS):
            rights = [right[k, j * PER : (j + 1) * PER].reshape(WIDE, TB) for k in (0, 1)]
            back_o[...] += dot(wide(grad2, j * WIDE // TB, WIDE // TB, here), rights[1])
            dense = contract_cols(latent[:here], rights[0]) + contract_cols(latent_o[...], rights[1])
            for b in range(WIDE // TB):
                n = j * (WIDE // TB) + b
                out[:, n * TB : (n + 1) * TB] = (dense[:, b * TB : (b + 1) * TB] + run[order[0, 3, n]]).astype(BF)
            yield
        for n in range(SLICES):
            running_sums(1, behind, n * 16 // SLICES)
            yield
        back_h = back_o[...].astype(BF)
        for j in range(4):
            lefts = [left[k, j * 16 : (j + 1) * 16].reshape(1024, TB) for k in (0, 1)]
            dense = contract_cols(back_c[:here], lefts[0]) + contract_cols(back_h, lefts[1])
            for b in range(8):
                n = j * 8 + b
                back_out[:, n * TB : (n + 1) * TB] = (dense[:, b * TB : (b + 1) * TB] + run[order[1, 3, n]]).astype(BF)
            if j % 2:
                yield

    run_with(list(runs[:3]), work())
    runs[3]()


def products(places, order, same, full, tok, tok_s, grad, grad_s, scale):
    here = tok.shape[0]
    return pl.pallas_call(
        lambda *refs: products_kernel(scale, *refs),
        out_shape=(
            jax.ShapeDtypeStruct((2, QROWS, TB), F32),
            jax.ShapeDtypeStruct((here, FF), BF),
            jax.ShapeDtypeStruct((here, D), BF),
        ),
        in_specs=[pl.BlockSpec(memory_space=pltpu.SMEM)] * 3 + [ANY] * 5,
        out_specs=(VMEM,) * 3,
        scratch_shapes=[
            pltpu.VMEM((SIDE, SIDE, SIDE, QROWS, TB), BF),
            pltpu.VMEM((2, 64, LEFT, TB), BF),
            pltpu.VMEM((2, 64, RIGHT, TB), BF),
            pltpu.VMEM((2, 64, TB, TB), BF),
            pltpu.VMEM((D // TB, 2 * here, TB), BF),
            pltpu.VMEM((FF // TB, 2 * here, TB), BF),
            pltpu.VMEM((EMPTY + 1, here, TB), F32),
            pltpu.VMEM((2 * here, TB), BF),
            pltpu.VMEM((here, TB), BF),
            pltpu.VMEM((2 * here, TB), BF),
            pltpu.VMEM((here, TB), F32),
            pltpu.VMEM((3, 2 * here, PIECE), BF),
            pltpu.SemaphoreType.DMA((2,)),
            pltpu.SemaphoreType.DMA((2,)),
            pltpu.SemaphoreType.DMA,
            pltpu.SemaphoreType.DMA((2, 3)),
            pltpu.SemaphoreType.DMA((80,)),
            pltpu.SemaphoreType.DMA((80,)),
        ]
        + reduce_scratch(),
        compiler_params=pltpu.CompilerParams(
            collective_id=1, has_side_effects=True, vmem_limit_bytes=62 * 1024 * 1024
        ),
        name="products_and_reduction",
    )(places, order, same, full, tok, tok_s, grad, grad_s)


def sorted_tiles(places):
    ids = jnp.arange(128, dtype=jnp.int32)
    found, joins = [], []
    for key, other in ((places[1], places[0]), (places[0], places[1])):
        unique = key * 128 + ids
        rank = jnp.sum((unique[None, :] < unique[:, None]).astype(jnp.int32), 1)
        at = rank[None, :] == ids[:, None]
        pick = lambda v: jnp.sum(jnp.where(at, v[None, :], 0), 1)
        by = pick(key)
        joins.append(jnp.concatenate([jnp.zeros((1,), F32), (by[1:] == by[:-1]).astype(F32)]))
        upto = jnp.sum((key[None, :] <= ids[:, None]).astype(jnp.int32), 1)
        present = jnp.any(key[None, :] == ids[:, None], 1)
        found.append(jnp.stack([pick(other), pick(ids % 2), pick(ids // 2), jnp.where(present, upto - 1, EMPTY)]))
    return jnp.stack(found), jnp.stack(joins)


def local(tokens, left_factor, right_factor, tile_values, tile_rows, tile_cols, grad_out):
    grad_scale = 1.0 / math.sqrt(tokens.shape[0] * lax.axis_size("fsdp") * lax.axis_size("rep"))
    places = jnp.stack([tile_rows, tile_cols], 1).astype(BF)
    pay = jnp.concatenate(
        [
            left_factor.reshape(LEFT, 2, TB).transpose(1, 0, 2),
            right_factor.T.reshape(RIGHT, 2, TB).transpose(1, 0, 2),
            tile_values,
            jnp.broadcast_to(jnp.pad(places, ((0, 0), (0, TB - 2)))[:, None, :], (2, 16, TB)),
        ],
        1,
    )
    full, tok_s, grad_s = gather(pay, tokens, grad_out)
    full = full.reshape(2, 64, GROWS, TB)
    places_all = full[:, :, QROWS, :2].astype(jnp.int32).transpose(2, 1, 0).reshape(2, 128)
    total, out_rows, input_grad = products(
        places_all, *sorted_tiles(places_all), full, tokens, tok_s, grad_out, grad_s, grad_scale
    )
    left_grad = total[:, :LEFT].transpose(1, 0, 2).reshape(LEFT, R)
    right_grad = total[:, LEFT : LEFT + RIGHT].transpose(0, 2, 1).reshape(R, RIGHT)
    return (out_rows, input_grad, left_grad, right_grad, total[:, LEFT + RIGHT :])


def solution(mesh):
    placed = (
        P(("rep", "fsdp"), None),
        P("fsdp", None),
        P(None, "fsdp"),
        P("fsdp", None, None),
        P("fsdp"),
        P("fsdp"),
        P(("rep", "fsdp"), None),
    )
    return jax.shard_map(
        local,
        mesh=mesh,
        in_specs=placed,
        out_specs=(
            P(("rep", "fsdp"), None),
            P(("rep", "fsdp"), None),
            P("fsdp", None),
            P(None, "fsdp"),
            P("fsdp", None, None),
        ),
        check_vma=False,
    )
```

```python
import math

import jax
import jax.numpy as jnp
from jax import lax
from jax.experimental import pallas as pl
from jax.experimental.pallas import tpu as pltpu
from jax.sharding import PartitionSpec as P

D = 4096
FF = 14336
TB = 128
R = 256
SIDE = 4
LEFT = 64
RIGHT = 224
QROWS = LEFT + RIGHT + TB
MESH = pl.DeviceIdType.MESH
BF = jnp.bfloat16
F32 = jnp.float32
Y, H, X = 0, 1, 2
ANY = pl.BlockSpec(memory_space=pl.ANY)
VMEM = pl.BlockSpec(memory_space=pltpu.VMEM)


class Place:
    def __init__(self):
        rep, f = lax.axis_index("rep"), lax.axis_index("fsdp")
        self.l, self.c = rep // 2, rep % 2
        self.at = [f // 16, (f // 4) % 4, f % 4]
        self.s = 2 * self.l - 1
        self.sib = self.dev(core=1 - self.c)
        self.pair = self.dev(low=1 - self.l)
        self.out = self.dev(low=1 - self.l, step=(H, self.s))
        self.plus = {a: self.dev(step=(a, 1)) for a in (Y, X)}
        self.minus = {a: self.dev(step=(a, 3)) for a in (Y, X)}
        self.direct = {a: [self.dev(step=(a, k)) for k in (1, 3, 2)] for a in (Y, X)}
        self.direct[H] = [self.out, self.dev(step=(H, self.s)), self.dev(low=1 - self.l, step=(H, 2))]
        self.behind = self.dev(step=(H, -self.s))

    def dev(self, core=None, low=None, step=None):
        core = self.c if core is None else core
        low = self.l if low is None else low
        at = list(self.at)
        if step:
            at[step[0]] = (at[step[0]] + step[1] + 4) % 4
        return {"rep": low * 2 + core, "fsdp": (at[0] * 4 + at[1]) * 4 + at[2]}

    def greet(self):
        barrier = pltpu.get_barrier_semaphore()
        near = [self.sib, self.pair, self.behind] + [d for a in (Y, H, X) for d in self.direct[a]]
        for device in near:
            pl.semaphore_signal(barrier, inc=1, device_id=device, device_id_type=MESH)
        pl.semaphore_wait(barrier, len(near))


class Wire:
    def __init__(self, send_sems, recv_sems):
        self.send_sems, self.recv_sems = send_sems, recv_sems
        self.started = []

    def __call__(self, src, dst, device):
        k = len(self.started)
        copy = pltpu.make_async_remote_copy(
            src_ref=src,
            dst_ref=dst,
            send_sem=self.send_sems.at[k],
            recv_sem=self.recv_sems.at[k],
            device_id=device,
            device_id_type=MESH,
        )
        copy.start()
        self.started.append(copy)
        return copy

    def finish(self):
        for copy in self.started:
            copy.wait_send()


def view(ref, fixed, axis, j, row0, rows, half=None, chunk=None, chunks=1):
    sel = list(fixed)
    sel[axis] = j
    r0, n = row0, rows
    free = [a for a in range(3) if a != axis and fixed[a] is None]
    if half is not None:
        if free:
            width = 2 // chunks
            start = half * 2 + (0 if chunk is None else chunk * width)
            sel[free[0]] = pl.ds(start, width if chunk is not None else 2)
        elif rows % 32 == 0:
            n = rows // 2
            r0 = row0 + half * n
        else:
            cut = (rows // 32 + 1) * 16
            r0, n = (row0, cut) if half == 0 else (row0 + cut, rows - cut)
    sel = [slice(None) if v is None else v for v in sel]
    return ref.at[sel[0], sel[1], sel[2], pl.ds(r0, n), :]


GATHER = (((X, Y, H), 0, 128), ((Y, H, X), 128, 144), ((H, X, Y), 272, 144))


def spread(me, axis, send, got, ready):
    i = me.at[axis]
    across = (i + 2) % 4
    if axis == H:
        l, s = me.l, me.s
        up, down = (i + s + 4) % 4, (i - s + 4) % 4
        a, b = send(i, 1 - l, me.out), send(i, l, me.out)
        yield
        a.wait_recv()
        f = send(up, l, me.pair)
        got(up, l)
        yield
        b.wait_recv()
        e = send(up, 1 - l, me.pair)
        got(up, 1 - l)
        ready(up)
        yield
        f.wait_recv()
        g = send(down, 1 - l, me.out)
        got(down, 1 - l)
        yield
        e.wait_recv()
        got(down, l)
        ready(down)
        yield
        g.wait_recv()
        w = send(across, l, me.pair)
        got(across, l)
        yield
        w.wait_recv()
        got(across, 1 - l)
        ready(across)
    else:
        plus, minus = me.plus[axis], me.minus[axis]
        after, before = (i + 1) % 4, (i + 3) % 4
        a0, b1 = send(i, 0, plus), send(i, 1, minus)
        a1, b0 = send(i, 1, plus), send(i, 0, minus)
        yield
        a0.wait_recv()
        c0 = send(before, 0, plus)
        got(before, 0)
        b1.wait_recv()
        c1 = send(after, 1, minus)
        got(after, 1)
        yield
        a1.wait_recv()
        got(before, 1)
        ready(before)
        b0.wait_recv()
        got(after, 0)
        ready(after)
        yield
        c0.wait_recv()
        got(across, 0)
        c1.wait_recv()
        got(across, 1)
        ready(across)


REDUCE = (((H, Y, X), 0, 96), ((X, H, Y), 96, 96), ((Y, X, H), 192, 96), ((Y, X, H), 288, 128))


def add_into(dst, *terms):
    shape = dst.shape
    lead = shape[:-2]
    rows = shape[-2]
    count = math.prod(lead)

    def body(k, _):
        at = []
        for n in reversed(lead):
            at.append(k % n)
            k = k // n
        at = tuple(reversed(at))
        for r in range(0, rows, 16):
            here = at + (pl.ds(r, 16), slice(None))
            total = terms[0][here].astype(F32)
            for term in terms[1:]:
                total = total + term[here].astype(F32)
            dst[here] = total.astype(dst.dtype)
        return 0

    if count == 1:
        body(0, 0)
    else:
        lax.fori_loop(0, count, body, 0)


def reduce_parts(me, scale, q_ref, out, scratch):
    (send_sems, recv_sems), scratch = scratch[:2], scratch[2:]
    wire = Wire(send_sems, recv_sems)
    per_part = len(scratch) // len(REDUCE)

    def part(n):
        order, row0, rows = REDUCE[n]
        pool = list(scratch[n * per_part : (n + 1) * per_part])
        held = q_ref
        for stage, axis in enumerate(order):
            fixed = [me.at[a] if a in order[:stage] else None for a in range(3)]
            if stage:
                fixed = [0 if a in order[:stage] else None for a in range(3)]
            base = row0 if stage == 0 else 0
            staged = held
            nxt = pool.pop(0)
            first, second, third = pool.pop(0), pool.pop(0), pool.pop(0)
            dims = [a for a in range(3) if a != axis and fixed[a] is None]
            i = me.at[axis]

            def blk(ref, j, half=None, chunk=None, chunks=1):
                at0 = base if ref is held or ref is staged else 0
                return view(ref, fixed, axis, j, at0, rows, half, chunk, chunks)

            def send(j, half, dst, dst_j, device, extra=None, chunk=None, chunks=1):
                src = blk(staged, j, half, chunk, chunks)
                if extra is not None:
                    add_into(src, blk(held, j, half, chunk, chunks), extra)
                return wire(src, blk(dst, dst_j, half, chunk, chunks), device)

            if axis == H:
                l, s = me.l, me.s
                up, down, across = (i + s + 4) % 4, (i - s + 4) % 4, (i + 2) % 4
                chunks = 2 if stage == 0 else 1
                ids = range(chunks) if stage == 0 else (None,)
                a = [send(across, l, first, 0, me.pair, None, q, chunks) for q in ids]
                b = [send(down, 1 - l, second, 0, me.pair, None, q, chunks) for q in ids]
                yield
                c = []
                for k, q in enumerate(ids):
                    a[k].wait_recv()
                    c.append(send(across, 1 - l, first, 1, me.out, blk(first, 0, 1 - l, q, chunks), q, chunks))
                yield
                d = []
                for k, q in enumerate(ids):
                    b[k].wait_recv()
                    d.append(send(up, l, third, 0, me.out, blk(second, 0, l, q, chunks), q, chunks))
                yield
                e = []
                for k, q in enumerate(ids):
                    c[k].wait_recv()
                    e.append(send(down, l, second, 0, me.pair, blk(first, 1, l, q, chunks), q, chunks))
                yield
                f = []
                for k, q in enumerate(ids):
                    e[k].wait_recv()
                    f.append(send(up, 1 - l, third, 0, me.out, blk(second, 0, 1 - l, q, chunks), q, chunks))
                yield
                for k, q in enumerate(ids):
                    d[k].wait_recv()
                    add_into(blk(nxt, 0, 1 - l, q, chunks), blk(held, i, 1 - l, q, chunks), blk(third, 0, 1 - l, q, chunks))
                yield
                for k, q in enumerate(ids):
                    f[k].wait_recv()
                    add_into(blk(nxt, 0, l, q, chunks), blk(held, i, l, q, chunks), blk(third, 0, l, q, chunks))
            else:
                plus, minus = me.plus[axis], me.minus[axis]
                after, before, across = (i + 1) % 4, (i + 3) % 4, (i + 2) % 4
                a0 = send(across, 0, first, 0, plus)
                a1 = send(across, 1, first, 0, minus)
                b1 = send(after, 1, second, 0, plus)
                b0 = send(before, 0, third, 0, minus)
                yield
                a0.wait_recv()
                c0 = send(after, 0, second, 0, plus, blk(first, 0, 0))
                a1.wait_recv()
                c1 = send(before, 1, third, 0, minus, blk(first, 0, 1))
                yield
                b1.wait_recv()
                b0.wait_recv()
                yield
                c0.wait_recv()
                c1.wait_recv()
                for half in (0, 1):
                    add_into(blk(nxt, 0, half), blk(held, i, half), blk(second, 0, half), blk(third, 0, half))
            held = nxt
            yield
        other = pool.pop(0)
        swap = wire(held, other, me.pair)
        yield
        swap.wait_recv()
        place = out.at[me.c, pl.ds(row0, rows), :]
        place[...] = (held[0, 0, 0] + other[0, 0, 0]) * scale
        final = wire(place, place, me.sib)
        yield
        final.wait_recv()

    return [part(n) for n in range(len(REDUCE))] + [wire.finish]


def run_with(active, work):
    while active:
        for run in list(active):
            try:
                next(run)
            except StopIteration:
                active.remove(run)
        next(work, None)
    for _ in work:
        pass


def reduce_scratch():
    shapes = []
    for order, _, rows in REDUCE:
        dims = [SIDE] * 3
        for stage, axis in enumerate(order):
            wire = BF if stage < 1 else F32
            dims[axis] = 1
            shapes.append(pltpu.VMEM(tuple(dims) + (rows, TB), F32))
            two = list(dims)
            two[axis] = 2
            shapes.append(pltpu.VMEM(tuple(two if axis == H else dims) + (rows, TB), wire))
            shapes += [pltpu.VMEM(tuple(dims) + (rows, TB), wire)] * 2
        shapes.append(pltpu.VMEM((1, 1, 1, rows, TB), F32))
    return shapes


CHUNKS = 8
PER = 64 // CHUNKS
WIDE = PER * RIGHT
SLICES = 4
EMPTY = 128
PIECE = 2048


def contract_rows(left, right):
    return lax.dot_general(left, right, (((0,), (0,)), ((), ())), preferred_element_type=F32)


def contract_cols(left, right):
    return lax.dot_general(left, right, (((1,), (1,)), ((), ())), preferred_element_type=F32)


def dot(left, right):
    return jnp.dot(left, right, preferred_element_type=F32)


def wide(ref, first, count, rows=None):
    return jnp.concatenate([ref[n] if rows is None else ref[n, :rows] for n in range(first, first + count)], 1)


def load(src, dst, sem):
    copy = pltpu.make_async_copy(src, dst, sem)
    copy.start()
    return copy


def within(index, count):
    return jnp.minimum(jnp.maximum(index, 0), count - 1)


def sort_tiles(marks, order, joins):
    held = marks[...].reshape(64 * 16, TB)
    i0 = lax.broadcasted_iota(jnp.int32, (128, 1024), 0)
    i1 = lax.broadcasted_iota(jnp.int32, (128, 1024), 1)
    columns, rows = [], []
    for base in (0, 8):
        pick = (i1 == (i0 >> 1) * 16 + (i0 & 1) * 4 + base).astype(F32).astype(BF)
        columns.append(dot(pick, held))
        rows.append(lax.dot_general(held, pick, (((0,), (1,)), ((), ())), preferred_element_type=F32))
    t0 = lax.broadcasted_iota(jnp.int32, (128, 128), 0).astype(F32)
    t1 = lax.broadcasted_iota(jnp.int32, (128, 128), 1).astype(F32)
    s8 = lax.broadcasted_iota(jnp.int32, (8, 128), 0)
    lane = lax.broadcasted_iota(jnp.int32, (8, 128), 1)
    one = lambda truth: jnp.where(truth, 1.0, 0.0)
    for which, key in ((0, 1), (1, 0)):
        by0, by1, other = columns[key], rows[key], rows[1 - key]
        rank = jnp.sum(one(by1 * 128 + t1 < by0 * 128 + t0), 1, keepdims=True)
        moved = one(rank == t1).astype(BF)
        earlier = jnp.max(one(by0 == by1) * one(t0 < t1), 0, keepdims=True)
        upto = jnp.sum(one(by0 <= t1), 0, keepdims=True)
        present = jnp.max(one(by0 == t1), 0, keepdims=True)
        slot = jnp.where(present > 0.5, upto - 1, float(EMPTY))
        value = jnp.where(s8 == 0, other[:8], 0.0)
        value = jnp.where(s8 == 1, (lane & 1).astype(F32), value)
        value = jnp.where(s8 == 2, (lane >> 1).astype(F32), value)
        value = jnp.where(s8 == 4, jnp.broadcast_to(earlier, (8, 128)), value)
        found = dot(value.astype(BF), moved)
        found = jnp.where(s8 == 3, jnp.broadcast_to(slot, (8, 128)), found)
        order[which] = found.astype(jnp.int32)
        joins[which] = found
    order[2] = jnp.where(s8 == 0, rows[0][:8], rows[1][:8]).astype(jnp.int32)


def kernel(scale, pay, mark, tok, grad, total, out, back_out, full, tok_s, grad_s, *scratch):
    (q, left, right, tiles, tok2, grad2, run, latent, latent_o, back_c, back_o, stage, out_v, back_v) = scratch[:14]
    (marks, order_v, joins_v, order, joins) = scratch[14:19]
    left_sems, right_sems, tile_sem, stage_sems, order_sems, out_sem, back_sem = scratch[19:26]
    send_sems, recv_sems, local_sems, side_sems, wide_sems = scratch[26:31]
    me = Place()
    c, o = me.c, 1 - me.c
    here = tok.shape[0]
    mine = full.at[c]
    at = me.at
    own = [
        load(pay.at[c], mine.at[at[0], at[1], at[2]], local_sems.at[0]),
        load(mark, marks.at[at[0], at[1], at[2]], local_sems.at[1]),
    ]
    me.greet()
    for copy in own:
        copy.wait()
    wire = Wire(send_sems, recv_sems)
    active = []
    known = set()

    def to_sibling(src, dst, pair):
        return pltpu.make_async_remote_copy(
            src_ref=src,
            dst_ref=dst,
            send_sem=pair.at[0],
            recv_sem=pair.at[1],
            device_id=me.sib,
            device_id_type=MESH,
        )

    def positions():
        for seg, axis in (
            (marks.at[at[0], at[1], at[2]], H),
            (marks.at[at[0], :, at[2]], X),
            (marks.at[at[0]], Y),
        ):
            copies = [wire(seg, seg, device) for device in me.direct[axis]]
            yield
            for copy in copies:
                copy.wait_recv()
        known.add("marks")

    def part(order3, row0, rows):
        one, two, three = order3

        def piece(sel, half=None):
            sel = [sel.get(a, slice(None)) for a in range(3)]
            if half is not None:
                sel[one] = pl.ds(half * 2, 2)
            return mine.at[sel[0], sel[1], sel[2], pl.ds(row0, rows), :]

        def last(j2):
            def send(j, half, device):
                ref = piece({two: j2, three: j}, half)
                return wire(ref, ref, device)

            def got(j, half):
                ref = piece({two: j2, three: j}, half)
                to_sibling(ref, ref, side_sems).start()

            ref = piece({two: j2, three: at[three]})
            to_sibling(ref, ref, side_sems).start()
            return spread(me, three, send, got, lambda j: None)

        def start_last(j2):
            nonlocal_run = last(j2)
            next(nonlocal_run)
            active.append(nonlocal_run)

        def send(j, half, device):
            ref = piece({two: j, three: at[three]}, half)
            return wire(ref, ref, device)

        seed = piece({a: at[a] for a in range(3)})
        seeds = [wire(seed, seed, device) for device in me.direct[one]]
        yield
        for copy in seeds:
            copy.wait_recv()
        spreading = spread(me, two, send, lambda j, half: None, start_last)
        next(spreading)
        start_last(at[two])
        active.append(spreading)

    active.append(positions())
    for p in GATHER:
        active.append(part(*p))
    for each in active:
        next(each)
    swaps = [to_sibling(tok, tok_s, wide_sems.at[0]), to_sibling(grad, grad_s, wide_sems.at[1])]
    for swap in swaps:
        swap.start()
    sums = reduce_parts(me, scale, q, total, scratch[31:])
    pieces = [(tok, tok_s, tok2, n) for n in range(D // PIECE)] + [(grad, grad_s, grad2, n) for n in range(FF // PIECE)]

    def fetch(k):
        first, second, _, n = pieces[k]
        span = pl.ds(n * PIECE, PIECE)
        return [
            load(first.at[:, span], stage.at[k % 3, pl.ds(0, here)], stage_sems.at[0, k % 3]),
            load(second.at[:, span], stage.at[k % 3, pl.ds(here, here)], stage_sems.at[1, k % 3]),
        ]

    def tile_part(g, _):
        for u in range(8):
            t = 2 * (g * 8 + u) + c
            product = contract_rows(tok2[within(order[2, 0, t], D // TB)], grad2[within(order[2, 1, t], FF // TB)])
            q[g // 2, (g % 2) * 2 + u // 4, u % 4, LEFT + RIGHT :, :] = product.astype(BF)
        return 0

    def early():
        yield
        yield
        for swap in swaps:
            swap.wait_recv()
        coming = [fetch(k) for k in range(3)]
        for k, (_, _, held, n) in enumerate(pieces):
            for copy in coming[k]:
                copy.wait()
            for b in range(PIECE // TB):
                held[n * (PIECE // TB) + b] = stage[k % 3, :, b * TB : (b + 1) * TB]
            if k + 3 < len(pieces):
                coming.append(fetch(k + 3))
            if k % 3 == 2:
                yield
        while "marks" not in known:
            yield
        sort_tiles(marks, order_v, joins_v)
        filed = [load(order_v, order, order_sems.at[0]), load(joins_v, joins, order_sems.at[1])]
        for copy in filed:
            copy.wait()
        yield
        for n in range(2):
            lax.fori_loop(n * 4, n * 4 + 4, tile_part, 0)
            yield
        next(sums[3])
        summing.append(sums[3])

    summing = []
    before = early()
    while active:
        for each in list(active) + list(summing):
            if next(each, "end") == "end":
                (active if each in active else summing).remove(each)
        next(before, None)
    for _ in before:
        pass
    left_in = [load(full.at[c, :, :, :, pl.ds(0, LEFT), :], left.at[0], left_sems.at[0])]
    right_in = [load(full.at[c, :, :, :, pl.ds(LEFT, RIGHT), :], right.at[0], right_sems.at[0])]
    left_in[0].wait()
    latent[...] = dot(wide(tok2, 0, D // TB), left[0].reshape(D, TB)).astype(BF)
    right_in[0].wait()
    back = jnp.zeros((2 * here, TB), F32)
    for j in range(CHUNKS):
        cots = wide(grad2, j * WIDE // TB, WIDE // TB)
        y, h = j // 2, slice((j % 2) * 2, (j % 2) * 2 + 2)
        back = back + dot(cots, right[0, y, h].reshape(WIDE, TB))
        q[y, h, :, LEFT : LEFT + RIGHT, :] = contract_rows(cots, latent[...]).astype(BF).reshape(2, 4, RIGHT, TB)
    next(sums[1])
    next(sums[2])
    back_c[...] = back.astype(BF)
    for j in range(4):
        product = contract_rows(wide(tok2, j * 8, 8), back_c[...])
        q[j, :, :, :LEFT, :] = product.astype(BF).reshape(4, 4, LEFT, TB)
    next(sums[0])
    to_sibling(mine, full.at[o], side_sems).wait()
    left_in.append(load(full.at[o, :, :, :, pl.ds(0, LEFT), :], left.at[1], left_sems.at[1]))
    right_in.append(load(full.at[o, :, :, :, pl.ds(LEFT, RIGHT), :], right.at[1], right_sems.at[1]))
    for n in range(16):
        load(full.at[:, n // 4, n % 4, :, pl.ds(LEFT + RIGHT, TB), :], tiles.at[:, pl.ds(4 * n, 4)], tile_sem)
    tiles_in = pltpu.make_async_copy(tiles, tiles, tile_sem)

    def running_sums(which, product, g0):
        def body(g, held):
            parts = [product(g * 8 + u) for u in range(8)]
            for u in range(8):
                t = g * 8 + u
                held = held * joins[which, 4, t] + parts[u]
                run[t] = held
            return held

        first = jnp.zeros((here, TB), F32) if g0 == 0 else run[g0 * 8 - 1]
        lax.fori_loop(g0, g0 + 16 // SLICES, body, first)

    def tile(which, t):
        return tiles[within(order[which, 1, t], 2), within(order[which, 2, t], 64)]

    def ahead(t):
        return dot(tok2[within(order[0, 0, t], D // TB), :here], tile(0, t))

    def behind(t):
        return contract_cols(grad2[within(order[1, 0, t], FF // TB), :here], tile(1, t))

    def work():
        yield
        left_in[1].wait()
        latent_o[...] = dot(wide(tok2, 0, D // TB, here), left[1].reshape(D, TB)).astype(BF)
        tiles_in.wait()
        run[EMPTY] = jnp.zeros((here, TB), F32)
        for n in range(SLICES):
            running_sums(0, ahead, n * 16 // SLICES)
            yield
        right_in[1].wait()
        back_o[...] = jnp.zeros((here, TB), F32)
        for j in range(CHUNKS):
            span = slice(j * WIDE, (j + 1) * WIDE)
            y, h = j // 2, slice((j % 2) * 2, (j % 2) * 2 + 2)
            rights = [right[k, y, h].reshape(WIDE, TB) for k in (0, 1)]
            back_o[...] += dot(wide(grad2, j * WIDE // TB, WIDE // TB, here), rights[1])
            dense = contract_cols(latent[:here], rights[0]) + contract_cols(latent_o[...], rights[1])
            for b in range(WIDE // TB):
                n = j * (WIDE // TB) + b
                out_v[:, n * TB : (n + 1) * TB] = (dense[:, b * TB : (b + 1) * TB] + run[within(order[0, 3, n], EMPTY + 1)]).astype(BF)
            pltpu.make_async_copy(out_v.at[:, span], out.at[:, span], out_sem).start()
            yield
        for n in range(SLICES):
            running_sums(1, behind, n * 16 // SLICES)
            yield
        back_h = back_o[...].astype(BF)
        for j in range(4):
            lefts = [left[k, j].reshape(1024, TB) for k in (0, 1)]
            dense = contract_cols(back_c[:here], lefts[0]) + contract_cols(back_h, lefts[1])
            for b in range(8):
                n = j * 8 + b
                back_v[:, n * TB : (n + 1) * TB] = (dense[:, b * TB : (b + 1) * TB] + run[within(order[1, 3, n], EMPTY + 1)]).astype(BF)
            if j % 2:
                yield
        pltpu.make_async_copy(back_v, back_out, back_sem).start()

    run_with(summing + [sums[0], sums[1], sums[2]], work())
    pltpu.make_async_copy(out_v, out, out_sem).wait()
    pltpu.make_async_copy(back_v, back_out, back_sem).wait()
    wire.finish()
    for swap in swaps:
        swap.wait_send()
    sums[4]()


def whole_step(pay, mark, tok, grad, scale):
    here = tok.shape[0]
    return pl.pallas_call(
        lambda *refs: kernel(scale, *refs),
        out_shape=(
            jax.ShapeDtypeStruct((2, QROWS, TB), F32),
            jax.ShapeDtypeStruct((here, FF), BF),
            jax.ShapeDtypeStruct((here, D), BF),
            jax.ShapeDtypeStruct((2, SIDE, SIDE, SIDE, QROWS, TB), BF),
            jax.ShapeDtypeStruct(tok.shape, BF),
            jax.ShapeDtypeStruct(grad.shape, BF),
        ),
        in_specs=[ANY] * 4,
        out_specs=(VMEM,) + (ANY,) * 5,
        scratch_shapes=[
            pltpu.VMEM((SIDE, SIDE, SIDE, QROWS, TB), BF),
            pltpu.VMEM((2, SIDE, SIDE, SIDE, LEFT, TB), BF),
            pltpu.VMEM((2, SIDE, SIDE, SIDE, RIGHT, TB), BF),
            pltpu.VMEM((2, 64, TB, TB), BF),
            pltpu.VMEM((D // TB, 2 * here, TB), BF),
            pltpu.VMEM((FF // TB, 2 * here, TB), BF),
            pltpu.VMEM((EMPTY + 1, here, TB), F32),
            pltpu.VMEM((2 * here, TB), BF),
            pltpu.VMEM((here, TB), BF),
            pltpu.VMEM((2 * here, TB), BF),
            pltpu.VMEM((here, TB), F32),
            pltpu.VMEM((3, 2 * here, PIECE), BF),
            pltpu.VMEM((here, FF), BF),
            pltpu.VMEM((here, D), BF),
            pltpu.VMEM((SIDE, SIDE, SIDE, 16, TB), BF),
            pltpu.VMEM((3, 8, TB), jnp.int32),
            pltpu.VMEM((2, 8, TB), F32),
            pltpu.SMEM((3, 8, TB), jnp.int32),
            pltpu.SMEM((2, 8, TB), F32),
            pltpu.SemaphoreType.DMA((2,)),
            pltpu.SemaphoreType.DMA((2,)),
            pltpu.SemaphoreType.DMA,
            pltpu.SemaphoreType.DMA((2, 3)),
            pltpu.SemaphoreType.DMA((2,)),
            pltpu.SemaphoreType.DMA,
            pltpu.SemaphoreType.DMA,
            pltpu.SemaphoreType.DMA((120,)),
            pltpu.SemaphoreType.DMA((120,)),
            pltpu.SemaphoreType.DMA((2,)),
            pltpu.SemaphoreType.DMA((2,)),
            pltpu.SemaphoreType.DMA((2, 2)),
            pltpu.SemaphoreType.DMA((100,)),
            pltpu.SemaphoreType.DMA((100,)),
        ]
        + reduce_scratch(),
        compiler_params=pltpu.CompilerParams(
            collective_id=0, has_side_effects=True, vmem_limit_bytes=63 * 1024 * 1024
        ),
        name="whole_step",
    )(pay, mark, tok, grad)


def local(tokens, left_factor, right_factor, tile_values, tile_rows, tile_cols, grad_out):
    grad_scale = 1.0 / math.sqrt(tokens.shape[0] * lax.axis_size("fsdp") * lax.axis_size("rep"))
    mark = jnp.repeat(jnp.concatenate([tile_rows, tile_cols]).astype(BF), 4)
    mark = jnp.broadcast_to(mark[:, None], (16, TB))
    pay = jnp.concatenate(
        [
            left_factor.reshape(LEFT, 2, TB).transpose(1, 0, 2),
            right_factor.T.reshape(RIGHT, 2, TB).transpose(1, 0, 2),
            tile_values,
        ],
        1,
    )
    total, out_rows, input_grad, *_ = whole_step(pay, mark, tokens, grad_out, grad_scale)
    left_grad = total[:, :LEFT].transpose(1, 0, 2).reshape(LEFT, R)
    right_grad = total[:, LEFT : LEFT + RIGHT].transpose(0, 2, 1).reshape(R, RIGHT)
    return (out_rows, input_grad, left_grad, right_grad, total[:, LEFT + RIGHT :])


def solution(mesh):
    placed = (
        P(("rep", "fsdp"), None),
        P("fsdp", None),
        P(None, "fsdp"),
        P("fsdp", None, None),
        P("fsdp"),
        P("fsdp"),
        P(("rep", "fsdp"), None),
    )
    return jax.shard_map(
        local,
        mesh=mesh,
        in_specs=placed,
        out_specs=(
            P(("rep", "fsdp"), None),
            P(("rep", "fsdp"), None),
            P("fsdp", None),
            P(None, "fsdp"),
            P("fsdp", None, None),
        ),
        check_vma=False,
    )
```

```python
import math

import jax
import jax.numpy as jnp
from jax import lax
from jax.experimental import pallas as pl
from jax.experimental.pallas import tpu as pltpu
from jax.sharding import PartitionSpec as P

D = 4096
FF = 14336
TB = 128
R = 256
SIDE = 4
LEFT = 64
RIGHT = 224
QROWS = LEFT + RIGHT + TB
MESH = pl.DeviceIdType.MESH
BF = jnp.bfloat16
F32 = jnp.float32
Y, H, X = 0, 1, 2
ANY = pl.BlockSpec(memory_space=pl.ANY)
VMEM = pl.BlockSpec(memory_space=pltpu.VMEM)


class Place:
    def __init__(self):
        rep, f = lax.axis_index("rep"), lax.axis_index("fsdp")
        self.l, self.c = rep // 2, rep % 2
        self.at = [f // 16, (f // 4) % 4, f % 4]
        self.s = 2 * self.l - 1
        self.sib = self.dev(core=1 - self.c)
        self.pair = self.dev(low=1 - self.l)
        self.out = self.dev(low=1 - self.l, step=(H, self.s))
        self.plus = {a: self.dev(step=(a, 1)) for a in (Y, X)}
        self.minus = {a: self.dev(step=(a, 3)) for a in (Y, X)}
        self.direct = {a: [self.dev(step=(a, k)) for k in (1, 3, 2)] for a in (Y, X)}
        self.direct[H] = [self.out, self.dev(step=(H, self.s)), self.dev(low=1 - self.l, step=(H, 2))]
        self.behind = self.dev(step=(H, -self.s))

    def dev(self, core=None, low=None, step=None):
        core = self.c if core is None else core
        low = self.l if low is None else low
        at = list(self.at)
        if step:
            at[step[0]] = (at[step[0]] + step[1] + 4) % 4
        return {"rep": low * 2 + core, "fsdp": (at[0] * 4 + at[1]) * 4 + at[2]}

    def greet(self):
        barrier = pltpu.get_barrier_semaphore()
        near = [self.sib, self.pair, self.behind] + [d for a in (Y, H, X) for d in self.direct[a]]
        for device in near:
            pl.semaphore_signal(barrier, inc=1, device_id=device, device_id_type=MESH)
        pl.semaphore_wait(barrier, len(near))


class Wire:
    def __init__(self, send_sems, recv_sems):
        self.send_sems, self.recv_sems = send_sems, recv_sems
        self.started = []

    def __call__(self, src, dst, device):
        k = len(self.started)
        copy = pltpu.make_async_remote_copy(
            src_ref=src,
            dst_ref=dst,
            send_sem=self.send_sems.at[k],
            recv_sem=self.recv_sems.at[k],
            device_id=device,
            device_id_type=MESH,
        )
        copy.start()
        self.started.append(copy)
        return copy

    def finish(self):
        for copy in self.started:
            copy.wait_send()


def view(ref, fixed, axis, j, row0, rows, half=None, chunk=None, chunks=1):
    sel = list(fixed)
    sel[axis] = j
    r0, n = row0, rows
    free = [a for a in range(3) if a != axis and fixed[a] is None]
    if half is not None:
        if free:
            width = 2 // chunks
            start = half * 2 + (0 if chunk is None else chunk * width)
            sel[free[0]] = pl.ds(start, width if chunk is not None else 2)
        elif rows % 32 == 0:
            n = rows // 2
            r0 = row0 + half * n
        else:
            cut = (rows // 32 + 1) * 16
            r0, n = (row0, cut) if half == 0 else (row0 + cut, rows - cut)
    sel = [slice(None) if v is None else v for v in sel]
    return ref.at[sel[0], sel[1], sel[2], pl.ds(r0, n), :]


GATHER = (((X, Y, H), 0, 128), ((Y, H, X), 128, 144), ((H, X, Y), 272, 144))


def spread(me, axis, send, got, ready):
    i = me.at[axis]
    across = (i + 2) % 4
    if axis == H:
        l, s = me.l, me.s
        up, down = (i + s + 4) % 4, (i - s + 4) % 4
        a, b = send(i, 1 - l, me.out), send(i, l, me.out)
        yield
        a.wait_recv()
        f = send(up, l, me.pair)
        got(up, l)
        yield
        b.wait_recv()
        e = send(up, 1 - l, me.pair)
        got(up, 1 - l)
        ready(up)
        yield
        f.wait_recv()
        g = send(down, 1 - l, me.out)
        got(down, 1 - l)
        yield
        e.wait_recv()
        got(down, l)
        ready(down)
        yield
        g.wait_recv()
        w = send(across, l, me.pair)
        got(across, l)
        yield
        w.wait_recv()
        got(across, 1 - l)
        ready(across)
    else:
        plus, minus = me.plus[axis], me.minus[axis]
        after, before = (i + 1) % 4, (i + 3) % 4
        a0, b1 = send(i, 0, plus), send(i, 1, minus)
        a1, b0 = send(i, 1, plus), send(i, 0, minus)
        yield
        a0.wait_recv()
        c0 = send(before, 0, plus)
        got(before, 0)
        b1.wait_recv()
        c1 = send(after, 1, minus)
        got(after, 1)
        yield
        a1.wait_recv()
        got(before, 1)
        ready(before)
        b0.wait_recv()
        got(after, 0)
        ready(after)
        yield
        c0.wait_recv()
        got(across, 0)
        c1.wait_recv()
        got(across, 1)
        ready(across)


REDUCE = (((H, Y, X), 0, 96), ((X, H, Y), 96, 96), ((Y, X, H), 192, 96), ((Y, X, H), 288, 128))


def add_into(dst, *terms):
    shape = dst.shape
    lead = shape[:-2]
    rows = shape[-2]
    count = math.prod(lead)

    def body(k, _):
        at = []
        for n in reversed(lead):
            at.append(k % n)
            k = k // n
        at = tuple(reversed(at))
        for r in range(0, rows, 16):
            here = at + (pl.ds(r, 16), slice(None))
            total = terms[0][here].astype(F32)
            for term in terms[1:]:
                total = total + term[here].astype(F32)
            dst[here] = total.astype(dst.dtype)
        return 0

    if count == 1:
        body(0, 0)
    else:
        lax.fori_loop(0, count, body, 0)


def reduce_parts(me, scale, q_ref, out, scratch):
    (send_sems, recv_sems), scratch = scratch[:2], scratch[2:]
    wire = Wire(send_sems, recv_sems)
    per_part = len(scratch) // len(REDUCE)

    def part(n):
        order, row0, rows = REDUCE[n]
        pool = list(scratch[n * per_part : (n + 1) * per_part])
        held = q_ref
        for stage, axis in enumerate(order):
            fixed = [me.at[a] if a in order[:stage] else None for a in range(3)]
            if stage:
                fixed = [0 if a in order[:stage] else None for a in range(3)]
            base = row0 if stage == 0 else 0
            staged = held
            nxt = pool.pop(0)
            first, second, third = pool.pop(0), pool.pop(0), pool.pop(0)
            dims = [a for a in range(3) if a != axis and fixed[a] is None]
            i = me.at[axis]

            def blk(ref, j, half=None, chunk=None, chunks=1):
                at0 = base if ref is held or ref is staged else 0
                return view(ref, fixed, axis, j, at0, rows, half, chunk, chunks)

            def send(j, half, dst, dst_j, device, extra=None, chunk=None, chunks=1):
                src = blk(staged, j, half, chunk, chunks)
                if extra is not None:
                    add_into(src, blk(held, j, half, chunk, chunks), extra)
                return wire(src, blk(dst, dst_j, half, chunk, chunks), device)

            if axis == H:
                l, s = me.l, me.s
                up, down, across = (i + s + 4) % 4, (i - s + 4) % 4, (i + 2) % 4
                chunks = 2 if stage == 0 else 1
                ids = range(chunks) if stage == 0 else (None,)
                a = [send(across, l, first, 0, me.pair, None, q, chunks) for q in ids]
                b = [send(down, 1 - l, second, 0, me.pair, None, q, chunks) for q in ids]
                yield
                c = []
                for k, q in enumerate(ids):
                    a[k].wait_recv()
                    c.append(send(across, 1 - l, first, 1, me.out, blk(first, 0, 1 - l, q, chunks), q, chunks))
                yield
                d = []
                for k, q in enumerate(ids):
                    b[k].wait_recv()
                    d.append(send(up, l, third, 0, me.out, blk(second, 0, l, q, chunks), q, chunks))
                yield
                e = []
                for k, q in enumerate(ids):
                    c[k].wait_recv()
                    e.append(send(down, l, second, 0, me.pair, blk(first, 1, l, q, chunks), q, chunks))
                yield
                f = []
                for k, q in enumerate(ids):
                    e[k].wait_recv()
                    f.append(send(up, 1 - l, third, 0, me.out, blk(second, 0, 1 - l, q, chunks), q, chunks))
                yield
                for k, q in enumerate(ids):
                    d[k].wait_recv()
                    add_into(blk(nxt, 0, 1 - l, q, chunks), blk(held, i, 1 - l, q, chunks), blk(third, 0, 1 - l, q, chunks))
                yield
                for k, q in enumerate(ids):
                    f[k].wait_recv()
                    add_into(blk(nxt, 0, l, q, chunks), blk(held, i, l, q, chunks), blk(third, 0, l, q, chunks))
            else:
                plus, minus = me.plus[axis], me.minus[axis]
                after, before, across = (i + 1) % 4, (i + 3) % 4, (i + 2) % 4
                a0 = send(across, 0, first, 0, plus)
                a1 = send(across, 1, first, 0, minus)
                b1 = send(after, 1, second, 0, plus)
                b0 = send(before, 0, third, 0, minus)
                yield
                a0.wait_recv()
                c0 = send(after, 0, second, 0, plus, blk(first, 0, 0))
                a1.wait_recv()
                c1 = send(before, 1, third, 0, minus, blk(first, 0, 1))
                yield
                b1.wait_recv()
                b0.wait_recv()
                yield
                c0.wait_recv()
                c1.wait_recv()
                for half in (0, 1):
                    add_into(blk(nxt, 0, half), blk(held, i, half), blk(second, 0, half), blk(third, 0, half))
            held = nxt
            yield
        other = pool.pop(0)
        swap = wire(held, other, me.pair)
        yield
        swap.wait_recv()
        place = out.at[me.c, pl.ds(row0, rows), :]
        place[...] = (held[0, 0, 0] + other[0, 0, 0]) * scale
        final = wire(place, place, me.sib)
        yield
        final.wait_recv()

    return [part(n) for n in range(len(REDUCE))] + [wire.finish]


def run_with(active, work):
    while active:
        for run in list(active):
            try:
                next(run)
            except StopIteration:
                active.remove(run)
        next(work, None)
    for _ in work:
        pass


def reduce_scratch():
    shapes = []
    for order, _, rows in REDUCE:
        dims = [SIDE] * 3
        for stage, axis in enumerate(order):
            wire = BF if stage < 1 else F32
            dims[axis] = 1
            shapes.append(pltpu.VMEM(tuple(dims) + (rows, TB), F32))
            two = list(dims)
            two[axis] = 2
            shapes.append(pltpu.VMEM(tuple(two if axis == H else dims) + (rows, TB), wire))
            shapes += [pltpu.VMEM(tuple(dims) + (rows, TB), wire)] * 2
        shapes.append(pltpu.VMEM((1, 1, 1, rows, TB), F32))
    return shapes


CHUNKS = 8
PER = 64 // CHUNKS
WIDE = PER * RIGHT
SLICES = 4
EMPTY = 128
PIECE = 2048


def contract_rows(left, right):
    return lax.dot_general(left, right, (((0,), (0,)), ((), ())), preferred_element_type=F32)


def contract_cols(left, right):
    return lax.dot_general(left, right, (((1,), (1,)), ((), ())), preferred_element_type=F32)


def dot(left, right):
    return jnp.dot(left, right, preferred_element_type=F32)


def wide(ref, first, count, rows=None):
    return jnp.concatenate([ref[n] if rows is None else ref[n, :rows] for n in range(first, first + count)], 1)


def load(src, dst, sem):
    copy = pltpu.make_async_copy(src, dst, sem)
    copy.start()
    return copy


def within(index, count):
    return jnp.minimum(jnp.maximum(index, 0), count - 1)


def sort_tiles(marks, order, joins):
    held = marks[...].reshape(64 * 16, TB)
    i0 = lax.broadcasted_iota(jnp.int32, (128, 1024), 0)
    i1 = lax.broadcasted_iota(jnp.int32, (128, 1024), 1)
    columns, rows = [], []
    for base in (0, 8):
        pick = (i1 == (i0 >> 1) * 16 + (i0 & 1) * 4 + base).astype(F32).astype(BF)
        columns.append(dot(pick, held))
        rows.append(lax.dot_general(held, pick, (((0,), (1,)), ((), ())), preferred_element_type=F32))
    t0 = lax.broadcasted_iota(jnp.int32, (128, 128), 0).astype(F32)
    t1 = lax.broadcasted_iota(jnp.int32, (128, 128), 1).astype(F32)
    s8 = lax.broadcasted_iota(jnp.int32, (8, 128), 0)
    lane = lax.broadcasted_iota(jnp.int32, (8, 128), 1)
    one = lambda truth: jnp.where(truth, 1.0, 0.0)
    for which, key in ((0, 1), (1, 0)):
        by0, by1, other = columns[key], rows[key], rows[1 - key]
        rank = jnp.sum(one(by1 * 128 + t1 < by0 * 128 + t0), 1, keepdims=True)
        moved = one(rank == t1).astype(BF)
        earlier = jnp.max(one(by0 == by1) * one(t0 < t1), 0, keepdims=True)
        upto = jnp.sum(one(by0 <= t1), 0, keepdims=True)
        present = jnp.max(one(by0 == t1), 0, keepdims=True)
        slot = jnp.where(present > 0.5, upto - 1, float(EMPTY))
        value = jnp.where(s8 == 0, other[:8], 0.0)
        value = jnp.where(s8 == 1, (lane & 1).astype(F32), value)
        value = jnp.where(s8 == 2, (lane >> 1).astype(F32), value)
        value = jnp.where(s8 == 4, jnp.broadcast_to(earlier, (8, 128)), value)
        found = dot(value.astype(BF), moved)
        found = jnp.where(s8 == 3, jnp.broadcast_to(slot, (8, 128)), found)
        order[which] = found.astype(jnp.int32)
        joins[which] = found
    order[2] = jnp.where(s8 == 0, rows[0][:8], rows[1][:8]).astype(jnp.int32)


def kernel(scale, tile_rows, tile_cols, left_own, right_own, tiles_own, tok, grad, out, back_out, left_grad, right_grad, tile_grad, full, tok_s, grad_s, *scratch):
    (q, left, right, tiles, tok2, grad2, run, latent, latent_o, back_c, back_o, stage, out_v, back_v) = scratch[:14]
    (marks, order_v, joins_v, order, joins) = scratch[14:19]
    left_sems, right_sems, tile_sem, stage_sems, order_sems, out_sem, back_sem = scratch[19:26]
    send_sems, recv_sems, local_sems, side_sems, wide_sems = scratch[26:31]
    me = Place()
    c, o = me.c, 1 - me.c
    here = tok.shape[0]
    mine = full.at[c]
    at = me.at
    pay, total = scratch[31:33]
    pay[:LEFT] = jnp.where(c == 0, left_own[:, :TB], left_own[:, TB:])
    turned = right_own[pl.ds(pl.multiple_of(c * TB, TB), TB), :].astype(F32)
    turned = jnp.concatenate([turned, jnp.zeros((TB, 2 * TB - RIGHT), F32)], 1).T
    pay[LEFT : LEFT + RIGHT] = turned[:RIGHT].astype(BF)
    pay[LEFT + RIGHT :] = tiles_own[c]
    found = [ref[k].astype(F32) for ref in (tile_rows, tile_cols) for k in (0, 1)]
    group = lax.broadcasted_iota(jnp.int32, (16, TB), 0) // 4
    mark = jnp.full((16, TB), found[3], F32)
    for k in (2, 1, 0):
        mark = jnp.where(group == k, found[k], mark)
    marks[at[0], at[1], at[2]] = mark.astype(BF)
    own = load(pay, mine.at[at[0], at[1], at[2]], local_sems.at[0])
    me.greet()
    own.wait()
    wire = Wire(send_sems, recv_sems)
    active = []
    known = set()

    def to_sibling(src, dst, pair):
        return pltpu.make_async_remote_copy(
            src_ref=src,
            dst_ref=dst,
            send_sem=pair.at[0],
            recv_sem=pair.at[1],
            device_id=me.sib,
            device_id_type=MESH,
        )

    def positions():
        for seg, axis in (
            (marks.at[at[0], at[1], at[2]], H),
            (marks.at[at[0], :, at[2]], X),
            (marks.at[at[0]], Y),
        ):
            copies = [wire(seg, seg, device) for device in me.direct[axis]]
            yield
            for copy in copies:
                copy.wait_recv()
        known.add("marks")

    def part(order3, row0, rows):
        one, two, three = order3

        def piece(sel, half=None):
            sel = [sel.get(a, slice(None)) for a in range(3)]
            if half is not None:
                sel[one] = pl.ds(half * 2, 2)
            return mine.at[sel[0], sel[1], sel[2], pl.ds(row0, rows), :]

        def last(j2):
            def send(j, half, device):
                ref = piece({two: j2, three: j}, half)
                return wire(ref, ref, device)

            def got(j, half):
                ref = piece({two: j2, three: j}, half)
                to_sibling(ref, ref, side_sems).start()

            ref = piece({two: j2, three: at[three]})
            to_sibling(ref, ref, side_sems).start()
            return spread(me, three, send, got, lambda j: None)

        def start_last(j2):
            nonlocal_run = last(j2)
            next(nonlocal_run)
            active.append(nonlocal_run)

        def send(j, half, device):
            ref = piece({two: j, three: at[three]}, half)
            return wire(ref, ref, device)

        seed = piece({a: at[a] for a in range(3)})
        seeds = [wire(seed, seed, device) for device in me.direct[one]]
        yield
        for copy in seeds:
            copy.wait_recv()
        spreading = spread(me, two, send, lambda j, half: None, start_last)
        next(spreading)
        start_last(at[two])
        active.append(spreading)

    active.append(positions())
    for p in GATHER:
        active.append(part(*p))
    for each in active:
        next(each)
    swaps = [to_sibling(tok, tok_s, wide_sems.at[0]), to_sibling(grad, grad_s, wide_sems.at[1])]
    for swap in swaps:
        swap.start()
    sums = reduce_parts(me, scale, q, total, scratch[33:])
    pieces = [(tok, tok_s, tok2, n) for n in range(D // PIECE)] + [(grad, grad_s, grad2, n) for n in range(FF // PIECE)]

    def fetch(k):
        first, second, _, n = pieces[k]
        span = pl.ds(n * PIECE, PIECE)
        return [
            load(first.at[:, span], stage.at[k % 3, pl.ds(0, here)], stage_sems.at[0, k % 3]),
            load(second.at[:, span], stage.at[k % 3, pl.ds(here, here)], stage_sems.at[1, k % 3]),
        ]

    def tile_part(g, _):
        for u in range(8):
            t = 2 * (g * 8 + u) + c
            product = contract_rows(tok2[within(order[2, 0, t], D // TB)], grad2[within(order[2, 1, t], FF // TB)])
            q[g // 2, (g % 2) * 2 + u // 4, u % 4, LEFT + RIGHT :, :] = product.astype(BF)
        return 0

    def early():
        yield
        yield
        for swap in swaps:
            swap.wait_recv()
        coming = [fetch(k) for k in range(3)]
        for k, (_, _, held, n) in enumerate(pieces):
            for copy in coming[k]:
                copy.wait()
            for b in range(PIECE // TB):
                held[n * (PIECE // TB) + b] = stage[k % 3, :, b * TB : (b + 1) * TB]
            if k + 3 < len(pieces):
                coming.append(fetch(k + 3))
            if k % 3 == 2:
                yield
        while "marks" not in known:
            yield
        sort_tiles(marks, order_v, joins_v)
        filed = [load(order_v, order, order_sems.at[0]), load(joins_v, joins, order_sems.at[1])]
        for copy in filed:
            copy.wait()
        yield
        for n in range(2):
            lax.fori_loop(n * 4, n * 4 + 4, tile_part, 0)
            yield
        next(sums[3])
        summing.append(sums[3])

    summing = []
    before = early()
    while active:
        for each in list(active) + list(summing):
            if next(each, "end") == "end":
                (active if each in active else summing).remove(each)
        next(before, None)
    for _ in before:
        pass
    left_in = [load(full.at[c, :, :, :, pl.ds(0, LEFT), :], left.at[0], left_sems.at[0])]
    right_in = [load(full.at[c, :, :, :, pl.ds(LEFT, RIGHT), :], right.at[0], right_sems.at[0])]
    left_in[0].wait()
    latent[...] = dot(wide(tok2, 0, D // TB), left[0].reshape(D, TB)).astype(BF)
    right_in[0].wait()
    back = jnp.zeros((2 * here, TB), F32)
    for j in range(CHUNKS):
        cots = wide(grad2, j * WIDE // TB, WIDE // TB)
        y, h = j // 2, slice((j % 2) * 2, (j % 2) * 2 + 2)
        back = back + dot(cots, right[0, y, h].reshape(WIDE, TB))
        q[y, h, :, LEFT : LEFT + RIGHT, :] = contract_rows(cots, latent[...]).astype(BF).reshape(2, 4, RIGHT, TB)
    next(sums[1])
    next(sums[2])
    back_c[...] = back.astype(BF)
    for j in range(4):
        product = contract_rows(wide(tok2, j * 8, 8), back_c[...])
        q[j, :, :, :LEFT, :] = product.astype(BF).reshape(4, 4, LEFT, TB)
    next(sums[0])
    to_sibling(mine, full.at[o], side_sems).wait()
    left_in.append(load(full.at[o, :, :, :, pl.ds(0, LEFT), :], left.at[1], left_sems.at[1]))
    right_in.append(load(full.at[o, :, :, :, pl.ds(LEFT, RIGHT), :], right.at[1], right_sems.at[1]))
    for n in range(16):
        load(full.at[:, n // 4, n % 4, :, pl.ds(LEFT + RIGHT, TB), :], tiles.at[:, pl.ds(4 * n, 4)], tile_sem)
    tiles_in = pltpu.make_async_copy(tiles, tiles, tile_sem)

    def running_sums(which, product, g0):
        def body(g, held):
            parts = [product(g * 8 + u) for u in range(8)]
            for u in range(8):
                t = g * 8 + u
                held = held * joins[which, 4, t] + parts[u]
                run[t] = held
            return held

        first = jnp.zeros((here, TB), F32) if g0 == 0 else run[g0 * 8 - 1]
        lax.fori_loop(g0, g0 + 16 // SLICES, body, first)

    def tile(which, t):
        return tiles[within(order[which, 1, t], 2), within(order[which, 2, t], 64)]

    def ahead(t):
        return dot(tok2[within(order[0, 0, t], D // TB), :here], tile(0, t))

    def behind(t):
        return contract_cols(grad2[within(order[1, 0, t], FF // TB), :here], tile(1, t))

    def work():
        yield
        left_in[1].wait()
        latent_o[...] = dot(wide(tok2, 0, D // TB, here), left[1].reshape(D, TB)).astype(BF)
        tiles_in.wait()
        run[EMPTY] = jnp.zeros((here, TB), F32)
        for n in range(SLICES):
            running_sums(0, ahead, n * 16 // SLICES)
            yield
        right_in[1].wait()
        back_o[...] = jnp.zeros((here, TB), F32)
        for j in range(CHUNKS):
            span = slice(j * WIDE, (j + 1) * WIDE)
            y, h = j // 2, slice((j % 2) * 2, (j % 2) * 2 + 2)
            rights = [right[k, y, h].reshape(WIDE, TB) for k in (0, 1)]
            back_o[...] += dot(wide(grad2, j * WIDE // TB, WIDE // TB, here), rights[1])
            dense = contract_cols(latent[:here], rights[0]) + contract_cols(latent_o[...], rights[1])
            for b in range(WIDE // TB):
                n = j * (WIDE // TB) + b
                out_v[:, n * TB : (n + 1) * TB] = (dense[:, b * TB : (b + 1) * TB] + run[within(order[0, 3, n], EMPTY + 1)]).astype(BF)
            pltpu.make_async_copy(out_v.at[:, span], out.at[:, span], out_sem).start()
            yield
        for n in range(SLICES):
            running_sums(1, behind, n * 16 // SLICES)
            yield
        back_h = back_o[...].astype(BF)
        for j in range(4):
            lefts = [left[k, j].reshape(1024, TB) for k in (0, 1)]
            dense = contract_cols(back_c[:here], lefts[0]) + contract_cols(back_h, lefts[1])
            for b in range(8):
                n = j * 8 + b
                back_v[:, n * TB : (n + 1) * TB] = (dense[:, b * TB : (b + 1) * TB] + run[within(order[1, 3, n], EMPTY + 1)]).astype(BF)
            if j % 2:
                yield
        pltpu.make_async_copy(back_v, back_out, back_sem).start()

    run_with(summing + [sums[0], sums[1], sums[2]], work())
    pltpu.make_async_copy(out_v, out, out_sem).wait()
    pltpu.make_async_copy(back_v, back_out, back_sem).wait()
    wire.finish()
    for swap in swaps:
        swap.wait_send()
    sums[4]()
    for k in (0, 1):
        half = slice(k * TB, (k + 1) * TB)
        left_grad[:, half] = total[k, :LEFT]
        right_grad[half, :] = total[k, LEFT : LEFT + 2 * TB].T[:, :RIGHT]
        tile_grad[k] = total[k, LEFT + RIGHT :]


def whole_step(rows, cols, left, right, tiles, tok, grad, scale):
    here = tok.shape[0]
    return pl.pallas_call(
        lambda *refs: kernel(scale, *refs),
        out_shape=(
            jax.ShapeDtypeStruct((here, FF), BF),
            jax.ShapeDtypeStruct((here, D), BF),
            jax.ShapeDtypeStruct((LEFT, R), F32),
            jax.ShapeDtypeStruct((R, RIGHT), F32),
            jax.ShapeDtypeStruct((2, TB, TB), F32),
            jax.ShapeDtypeStruct((2, SIDE, SIDE, SIDE, QROWS, TB), BF),
            jax.ShapeDtypeStruct(tok.shape, BF),
            jax.ShapeDtypeStruct(grad.shape, BF),
        ),
        in_specs=[pl.BlockSpec(memory_space=pltpu.SMEM)] * 2 + [VMEM] * 3 + [ANY] * 2,
        out_specs=(ANY,) * 2 + (VMEM,) * 3 + (ANY,) * 3,
        scratch_shapes=[
            pltpu.VMEM((SIDE, SIDE, SIDE, QROWS, TB), BF),
            pltpu.VMEM((2, SIDE, SIDE, SIDE, LEFT, TB), BF),
            pltpu.VMEM((2, SIDE, SIDE, SIDE, RIGHT, TB), BF),
            pltpu.VMEM((2, 64, TB, TB), BF),
            pltpu.VMEM((D // TB, 2 * here, TB), BF),
            pltpu.VMEM((FF // TB, 2 * here, TB), BF),
            pltpu.VMEM((EMPTY + 1, here, TB), F32),
            pltpu.VMEM((2 * here, TB), BF),
            pltpu.VMEM((here, TB), BF),
            pltpu.VMEM((2 * here, TB), BF),
            pltpu.VMEM((here, TB), F32),
            pltpu.VMEM((3, 2 * here, PIECE), BF),
            pltpu.VMEM((here, FF), BF),
            pltpu.VMEM((here, D), BF),
            pltpu.VMEM((SIDE, SIDE, SIDE, 16, TB), BF),
            pltpu.VMEM((3, 8, TB), jnp.int32),
            pltpu.VMEM((2, 8, TB), F32),
            pltpu.SMEM((3, 8, TB), jnp.int32),
            pltpu.SMEM((2, 8, TB), F32),
            pltpu.SemaphoreType.DMA((2,)),
            pltpu.SemaphoreType.DMA((2,)),
            pltpu.SemaphoreType.DMA,
            pltpu.SemaphoreType.DMA((2, 3)),
            pltpu.SemaphoreType.DMA((2,)),
            pltpu.SemaphoreType.DMA,
            pltpu.SemaphoreType.DMA,
            pltpu.SemaphoreType.DMA((120,)),
            pltpu.SemaphoreType.DMA((120,)),
            pltpu.SemaphoreType.DMA((2,)),
            pltpu.SemaphoreType.DMA((2,)),
            pltpu.SemaphoreType.DMA((2, 2)),
            pltpu.VMEM((QROWS, TB), BF),
            pltpu.VMEM((2, QROWS, TB), F32),
            pltpu.SemaphoreType.DMA((100,)),
            pltpu.SemaphoreType.DMA((100,)),
        ]
        + reduce_scratch(),
        compiler_params=pltpu.CompilerParams(
            collective_id=0, has_side_effects=True, vmem_limit_bytes=63 * 1024 * 1024
        ),
        name="whole_step",
    )(rows, cols, left, right, tiles, tok, grad)


def local(tokens, left_factor, right_factor, tile_values, tile_rows, tile_cols, grad_out):
    grad_scale = 1.0 / math.sqrt(tokens.shape[0] * lax.axis_size("fsdp") * lax.axis_size("rep"))
    return tuple(
        whole_step(tile_rows, tile_cols, left_factor, right_factor, tile_values, tokens, grad_out, grad_scale)[:5]
    )


def solution(mesh):
    placed = (
        P(("rep", "fsdp"), None),
        P("fsdp", None),
        P(None, "fsdp"),
        P("fsdp", None, None),
        P("fsdp"),
        P("fsdp"),
        P(("rep", "fsdp"), None),
    )
    return jax.shard_map(
        local,
        mesh=mesh,
        in_specs=placed,
        out_specs=(
            P(("rep", "fsdp"), None),
            P(("rep", "fsdp"), None),
            P("fsdp", None),
            P(None, "fsdp"),
            P("fsdp", None, None),
        ),
        check_vma=False,
    )
```

```python
import math

import jax
import jax.numpy as jnp
from jax import lax
from jax.experimental import pallas as pl
from jax.experimental.pallas import tpu as pltpu
from jax.sharding import PartitionSpec as P

D = 4096
FF = 14336
TB = 128
R = 256
SIDE = 4
LEFT = 64
RIGHT = 224
QROWS = LEFT + RIGHT + TB
MESH = pl.DeviceIdType.MESH
BF = jnp.bfloat16
F32 = jnp.float32
Y, H, X = 0, 1, 2
ANY = pl.BlockSpec(memory_space=pl.ANY)
VMEM = pl.BlockSpec(memory_space=pltpu.VMEM)


class Place:
    def __init__(self):
        rep, f = lax.axis_index("rep"), lax.axis_index("fsdp")
        self.l, self.c = rep // 2, rep % 2
        self.at = [f // 16, (f // 4) % 4, f % 4]
        self.s = 2 * self.l - 1
        self.sib = self.dev(core=1 - self.c)
        self.pair = self.dev(low=1 - self.l)
        self.out = self.dev(low=1 - self.l, step=(H, self.s))
        self.plus = {a: self.dev(step=(a, 1)) for a in (Y, X)}
        self.minus = {a: self.dev(step=(a, 3)) for a in (Y, X)}
        self.direct = {a: [self.dev(step=(a, k)) for k in (1, 3, 2)] for a in (Y, X)}
        self.direct[H] = [self.out, self.dev(step=(H, self.s)), self.dev(low=1 - self.l, step=(H, 2))]
        self.behind = self.dev(step=(H, -self.s))

    def dev(self, core=None, low=None, step=None):
        core = self.c if core is None else core
        low = self.l if low is None else low
        at = list(self.at)
        if step:
            at[step[0]] = (at[step[0]] + step[1] + 4) % 4
        return {"rep": low * 2 + core, "fsdp": (at[0] * 4 + at[1]) * 4 + at[2]}

    def greet(self):
        barrier = pltpu.get_barrier_semaphore()
        near = [self.sib, self.pair, self.behind] + [d for a in (Y, H, X) for d in self.direct[a]]
        for device in near:
            pl.semaphore_signal(barrier, inc=1, device_id=device, device_id_type=MESH)
        pl.semaphore_wait(barrier, len(near))


class Wire:
    def __init__(self, send_sems, recv_sems):
        self.send_sems, self.recv_sems = send_sems, recv_sems
        self.started = []

    def __call__(self, src, dst, device):
        k = len(self.started)
        copy = pltpu.make_async_remote_copy(
            src_ref=src,
            dst_ref=dst,
            send_sem=self.send_sems.at[k],
            recv_sem=self.recv_sems.at[k],
            device_id=device,
            device_id_type=MESH,
        )
        copy.start()
        self.started.append(copy)
        return copy

    def finish(self):
        for copy in self.started:
            copy.wait_send()


def view(ref, fixed, axis, j, row0, rows, half=None, chunk=None, chunks=1):
    sel = list(fixed)
    sel[axis] = j
    r0, n = row0, rows
    free = [a for a in range(3) if a != axis and fixed[a] is None]
    if half is not None:
        if free:
            width = 2 // chunks
            start = half * 2 + (0 if chunk is None else chunk * width)
            sel[free[0]] = pl.ds(start, width if chunk is not None else 2)
        elif rows % 32 == 0:
            n = rows // 2
            r0 = row0 + half * n
        else:
            cut = (rows // 32 + 1) * 16
            r0, n = (row0, cut) if half == 0 else (row0 + cut, rows - cut)
    sel = [slice(None) if v is None else v for v in sel]
    return ref.at[sel[0], sel[1], sel[2], pl.ds(r0, n), :]


GATHER = (((X, Y, H), 0, 128), ((Y, H, X), 128, 144), ((H, X, Y), 272, 144))


def spread(me, axis, send, got, ready):
    i = me.at[axis]
    across = (i + 2) % 4
    if axis == H:
        l, s = me.l, me.s
        up, down = (i + s + 4) % 4, (i - s + 4) % 4
        a, b = send(i, 1 - l, me.out), send(i, l, me.out)
        yield
        a.wait_recv()
        f = send(up, l, me.pair)
        got(up, l)
        yield
        b.wait_recv()
        e = send(up, 1 - l, me.pair)
        got(up, 1 - l)
        ready(up)
        yield
        f.wait_recv()
        g = send(down, 1 - l, me.out)
        got(down, 1 - l)
        yield
        e.wait_recv()
        got(down, l)
        ready(down)
        yield
        g.wait_recv()
        w = send(across, l, me.pair)
        got(across, l)
        yield
        w.wait_recv()
        got(across, 1 - l)
        ready(across)
    else:
        plus, minus = me.plus[axis], me.minus[axis]
        after, before = (i + 1) % 4, (i + 3) % 4
        a0, b1 = send(i, 0, plus), send(i, 1, minus)
        a1, b0 = send(i, 1, plus), send(i, 0, minus)
        yield
        a0.wait_recv()
        c0 = send(before, 0, plus)
        got(before, 0)
        b1.wait_recv()
        c1 = send(after, 1, minus)
        got(after, 1)
        yield
        a1.wait_recv()
        got(before, 1)
        ready(before)
        b0.wait_recv()
        got(after, 0)
        ready(after)
        yield
        c0.wait_recv()
        got(across, 0)
        c1.wait_recv()
        got(across, 1)
        ready(across)


REDUCE = (((H, Y, X), 0, 96), ((X, H, Y), 96, 96), ((Y, X, H), 192, 96), ((Y, X, H), 288, 128))


def add_into(dst, *terms):
    shape = dst.shape
    lead = shape[:-2]
    rows = shape[-2]
    count = math.prod(lead)

    def body(k, _):
        at = []
        for n in reversed(lead):
            at.append(k % n)
            k = k // n
        at = tuple(reversed(at))
        for r in range(0, rows, 16):
            here = at + (pl.ds(r, 16), slice(None))
            total = terms[0][here].astype(F32)
            for term in terms[1:]:
                total = total + term[here].astype(F32)
            dst[here] = total.astype(dst.dtype)
        return 0

    if count == 1:
        body(0, 0)
    else:
        lax.fori_loop(0, count, body, 0)


def reduce_parts(me, scale, q_ref, out, scratch):
    (send_sems, recv_sems), scratch = scratch[:2], scratch[2:]
    wire = Wire(send_sems, recv_sems)
    per_part = len(scratch) // len(REDUCE)

    def part(n):
        order, row0, rows = REDUCE[n]
        pool = list(scratch[n * per_part : (n + 1) * per_part])
        held = q_ref
        for stage, axis in enumerate(order):
            fixed = [me.at[a] if a in order[:stage] else None for a in range(3)]
            if stage:
                fixed = [0 if a in order[:stage] else None for a in range(3)]
            base = row0 if stage == 0 else 0
            staged = held
            nxt = pool.pop(0)
            first, second, third = pool.pop(0), pool.pop(0), pool.pop(0)
            dims = [a for a in range(3) if a != axis and fixed[a] is None]
            i = me.at[axis]

            def blk(ref, j, half=None, chunk=None, chunks=1):
                at0 = base if ref is held or ref is staged else 0
                return view(ref, fixed, axis, j, at0, rows, half, chunk, chunks)

            def send(j, half, dst, dst_j, device, extra=None, chunk=None, chunks=1):
                src = blk(staged, j, half, chunk, chunks)
                if extra is not None:
                    add_into(src, blk(held, j, half, chunk, chunks), extra)
                return wire(src, blk(dst, dst_j, half, chunk, chunks), device)

            if axis == H:
                l, s = me.l, me.s
                up, down, across = (i + s + 4) % 4, (i - s + 4) % 4, (i + 2) % 4
                chunks = 2 if stage == 0 else 1
                ids = range(chunks) if stage == 0 else (None,)
                a = [send(across, l, first, 0, me.pair, None, q, chunks) for q in ids]
                b = [send(down, 1 - l, second, 0, me.pair, None, q, chunks) for q in ids]
                yield
                c = []
                for k, q in enumerate(ids):
                    a[k].wait_recv()
                    c.append(send(across, 1 - l, first, 1, me.out, blk(first, 0, 1 - l, q, chunks), q, chunks))
                yield
                d = []
                for k, q in enumerate(ids):
                    b[k].wait_recv()
                    d.append(send(up, l, third, 0, me.out, blk(second, 0, l, q, chunks), q, chunks))
                yield
                e = []
                for k, q in enumerate(ids):
                    c[k].wait_recv()
                    e.append(send(down, l, second, 0, me.pair, blk(first, 1, l, q, chunks), q, chunks))
                yield
                f = []
                for k, q in enumerate(ids):
                    e[k].wait_recv()
                    f.append(send(up, 1 - l, third, 0, me.out, blk(second, 0, 1 - l, q, chunks), q, chunks))
                yield
                for k, q in enumerate(ids):
                    d[k].wait_recv()
                    add_into(blk(nxt, 0, 1 - l, q, chunks), blk(held, i, 1 - l, q, chunks), blk(third, 0, 1 - l, q, chunks))
                yield
                for k, q in enumerate(ids):
                    f[k].wait_recv()
                    add_into(blk(nxt, 0, l, q, chunks), blk(held, i, l, q, chunks), blk(third, 0, l, q, chunks))
            else:
                plus, minus = me.plus[axis], me.minus[axis]
                after, before, across = (i + 1) % 4, (i + 3) % 4, (i + 2) % 4
                a0 = send(across, 0, first, 0, plus)
                a1 = send(across, 1, first, 0, minus)
                b1 = send(after, 1, second, 0, plus)
                b0 = send(before, 0, third, 0, minus)
                yield
                a0.wait_recv()
                c0 = send(after, 0, second, 0, plus, blk(first, 0, 0))
                a1.wait_recv()
                c1 = send(before, 1, third, 0, minus, blk(first, 0, 1))
                yield
                b1.wait_recv()
                b0.wait_recv()
                yield
                c0.wait_recv()
                c1.wait_recv()
                for half in (0, 1):
                    add_into(blk(nxt, 0, half), blk(held, i, half), blk(second, 0, half), blk(third, 0, half))
            held = nxt
            yield
        other = pool.pop(0)
        swap = wire(held, other, me.pair)
        yield
        swap.wait_recv()
        place = out.at[me.c, pl.ds(row0, rows), :]
        place[...] = (held[0, 0, 0] + other[0, 0, 0]) * scale
        final = wire(place, place, me.sib)
        yield
        final.wait_recv()

    return [part(n) for n in range(len(REDUCE))] + [wire.finish]


def run_with(active, work):
    while active:
        for run in list(active):
            try:
                next(run)
            except StopIteration:
                active.remove(run)
        next(work, None)
    for _ in work:
        pass


def reduce_scratch():
    shapes = []
    for order, _, rows in REDUCE:
        dims = [SIDE] * 3
        for stage, axis in enumerate(order):
            wire = BF if stage < 1 else F32
            dims[axis] = 1
            shapes.append(pltpu.VMEM(tuple(dims) + (rows, TB), F32))
            two = list(dims)
            two[axis] = 2
            shapes.append(pltpu.VMEM(tuple(two if axis == H else dims) + (rows, TB), wire))
            shapes += [pltpu.VMEM(tuple(dims) + (rows, TB), wire)] * 2
        shapes.append(pltpu.VMEM((1, 1, 1, rows, TB), F32))
    return shapes


CHUNKS = 8
PER = 64 // CHUNKS
WIDE = PER * RIGHT
SLICES = 2
EMPTY = 128
PIECE = 2048


def contract_rows(left, right):
    return lax.dot_general(left, right, (((0,), (0,)), ((), ())), preferred_element_type=F32)


def contract_cols(left, right):
    return lax.dot_general(left, right, (((1,), (1,)), ((), ())), preferred_element_type=F32)


def dot(left, right):
    return jnp.dot(left, right, preferred_element_type=F32)


def wide(ref, first, count, rows=None):
    return jnp.concatenate([ref[n] if rows is None else ref[n, :rows] for n in range(first, first + count)], 1)


def load(src, dst, sem):
    copy = pltpu.make_async_copy(src, dst, sem)
    copy.start()
    return copy


def within(index, count):
    return jnp.minimum(jnp.maximum(index, 0), count - 1)


def sort_tiles(marks, order, joins):
    held = marks[...].reshape(64 * 16, TB)
    i0 = lax.broadcasted_iota(jnp.int32, (128, 1024), 0)
    i1 = lax.broadcasted_iota(jnp.int32, (128, 1024), 1)
    columns, rows = [], []
    for base in (0, 8):
        pick = (i1 == (i0 >> 1) * 16 + (i0 & 1) * 4 + base).astype(F32).astype(BF)
        columns.append(dot(pick, held))
        rows.append(lax.dot_general(held, pick, (((0,), (1,)), ((), ())), preferred_element_type=F32))
    t0 = lax.broadcasted_iota(jnp.int32, (128, 128), 0).astype(F32)
    t1 = lax.broadcasted_iota(jnp.int32, (128, 128), 1).astype(F32)
    s8 = lax.broadcasted_iota(jnp.int32, (8, 128), 0)
    lane = lax.broadcasted_iota(jnp.int32, (8, 128), 1)
    one = lambda truth: jnp.where(truth, 1.0, 0.0)
    for which, key in ((0, 1), (1, 0)):
        by0, by1, other = columns[key], rows[key], rows[1 - key]
        rank = jnp.sum(one(by1 * 128 + t1 < by0 * 128 + t0), 1, keepdims=True)
        moved = one(rank == t1).astype(BF)
        earlier = jnp.max(one(by0 == by1) * one(t0 < t1), 0, keepdims=True)
        upto = jnp.sum(one(by0 <= t1), 0, keepdims=True)
        present = jnp.max(one(by0 == t1), 0, keepdims=True)
        slot = jnp.where(present > 0.5, upto - 1, float(EMPTY))
        value = jnp.where(s8 == 0, other[:8], 0.0)
        value = jnp.where(s8 == 1, (lane & 1).astype(F32), value)
        value = jnp.where(s8 == 2, (lane >> 1).astype(F32), value)
        value = jnp.where(s8 == 4, jnp.broadcast_to(earlier, (8, 128)), value)
        found = dot(value.astype(BF), moved)
        found = jnp.where(s8 == 3, jnp.broadcast_to(slot, (8, 128)), found)
        order[which] = found.astype(jnp.int32)
        joins[which] = found
    order[2] = jnp.where(s8 == 0, rows[0][:8], rows[1][:8]).astype(jnp.int32)


def kernel(scale, tile_rows, tile_cols, left_own, right_own, tiles_own, tok, grad, out, back_out, left_grad, right_grad, tile_grad, full, tok_s, grad_s, *scratch):
    (q, left, right, tiles, tok2, grad2, run, latent, latent_o, back_c, back_o, stage, out_v, back_v) = scratch[:14]
    (marks, order_v, joins_v, order, joins) = scratch[14:19]
    left_sems, right_sems, tile_sem, stage_sems, order_sems, out_sem, back_sem = scratch[19:26]
    send_sems, recv_sems, local_sems, side_sems, wide_sems = scratch[26:31]
    me = Place()
    c, o = me.c, 1 - me.c
    here = tok.shape[0]
    mine = full.at[c]
    at = me.at
    pay, total = scratch[31:33]
    pay[:LEFT] = jnp.where(c == 0, left_own[:, :TB], left_own[:, TB:])
    turned = right_own[pl.ds(pl.multiple_of(c * TB, TB), TB), :].astype(F32)
    turned = jnp.concatenate([turned, jnp.zeros((TB, 2 * TB - RIGHT), F32)], 1).T
    pay[LEFT : LEFT + RIGHT] = turned[:RIGHT].astype(BF)
    pay[LEFT + RIGHT :] = tiles_own[c]
    found = [ref[k].astype(F32) for ref in (tile_rows, tile_cols) for k in (0, 1)]
    group = lax.broadcasted_iota(jnp.int32, (16, TB), 0) // 4
    mark = jnp.full((16, TB), found[3], F32)
    for k in (2, 1, 0):
        mark = jnp.where(group == k, found[k], mark)
    marks[at[0], at[1], at[2]] = mark.astype(BF)
    own = load(pay, mine.at[at[0], at[1], at[2]], local_sems.at[0])
    me.greet()
    own.wait()
    wire = Wire(send_sems, recv_sems)
    active = []
    known = set()

    def to_sibling(src, dst, pair):
        return pltpu.make_async_remote_copy(
            src_ref=src,
            dst_ref=dst,
            send_sem=pair.at[0],
            recv_sem=pair.at[1],
            device_id=me.sib,
            device_id_type=MESH,
        )

    def positions():
        for seg, axis in (
            (marks.at[at[0], at[1], at[2]], H),
            (marks.at[at[0], :, at[2]], X),
            (marks.at[at[0]], Y),
        ):
            copies = [wire(seg, seg, device) for device in me.direct[axis]]
            yield
            for copy in copies:
                copy.wait_recv()
        known.add("marks")

    def part(order3, row0, rows):
        one, two, three = order3

        def piece(sel, half=None):
            sel = [sel.get(a, slice(None)) for a in range(3)]
            if half is not None:
                sel[one] = pl.ds(half * 2, 2)
            return mine.at[sel[0], sel[1], sel[2], pl.ds(row0, rows), :]

        def last(j2):
            def send(j, half, device):
                ref = piece({two: j2, three: j}, half)
                return wire(ref, ref, device)

            def got(j, half):
                ref = piece({two: j2, three: j}, half)
                to_sibling(ref, ref, side_sems).start()

            ref = piece({two: j2, three: at[three]})
            to_sibling(ref, ref, side_sems).start()
            return spread(me, three, send, got, lambda j: None)

        def start_last(j2):
            nonlocal_run = last(j2)
            next(nonlocal_run)
            active.append(nonlocal_run)

        def send(j, half, device):
            ref = piece({two: j, three: at[three]}, half)
            return wire(ref, ref, device)

        seed = piece({a: at[a] for a in range(3)})
        seeds = [wire(seed, seed, device) for device in me.direct[one]]
        yield
        for copy in seeds:
            copy.wait_recv()
        spreading = spread(me, two, send, lambda j, half: None, start_last)
        next(spreading)
        start_last(at[two])
        active.append(spreading)

    active.append(positions())
    for p in GATHER:
        active.append(part(*p))
    for each in active:
        next(each)
    swaps = [to_sibling(tok, tok_s, wide_sems.at[0]), to_sibling(grad, grad_s, wide_sems.at[1])]
    for swap in swaps:
        swap.start()
    sums = reduce_parts(me, scale, q, total, scratch[33:])
    pieces = [(tok, tok_s, tok2, n) for n in range(D // PIECE)] + [(grad, grad_s, grad2, n) for n in range(FF // PIECE)]

    def fetch(k):
        first, second, _, n = pieces[k]
        span = pl.ds(n * PIECE, PIECE)
        return [
            load(first.at[:, span], stage.at[k % 3, pl.ds(0, here)], stage_sems.at[0, k % 3]),
            load(second.at[:, span], stage.at[k % 3, pl.ds(here, here)], stage_sems.at[1, k % 3]),
        ]

    def tile_part(g, _):
        for u in range(8):
            t = 2 * (g * 8 + u) + c
            product = contract_rows(tok2[within(order[2, 0, t], D // TB)], grad2[within(order[2, 1, t], FF // TB)])
            q[g // 2, (g % 2) * 2 + u // 4, u % 4, LEFT + RIGHT :, :] = product.astype(BF)
        return 0

    def early():
        yield
        yield
        for swap in swaps:
            swap.wait_recv()
        coming = [fetch(k) for k in range(3)]
        for k, (_, _, held, n) in enumerate(pieces):
            for copy in coming[k]:
                copy.wait()
            for b in range(PIECE // TB):
                held[n * (PIECE // TB) + b] = stage[k % 3, :, b * TB : (b + 1) * TB]
            if k + 3 < len(pieces):
                coming.append(fetch(k + 3))
            if k % 3 == 2:
                yield
        while "marks" not in known:
            yield
        sort_tiles(marks, order_v, joins_v)
        filed = [load(order_v, order, order_sems.at[0]), load(joins_v, joins, order_sems.at[1])]
        for copy in filed:
            copy.wait()
        yield
        for n in range(2):
            lax.fori_loop(n * 4, n * 4 + 4, tile_part, 0)
            yield
        next(sums[3])
        summing.append(sums[3])

    summing = []
    before = early()
    while active:
        for each in list(active) + list(summing):
            if next(each, "end") == "end":
                (active if each in active else summing).remove(each)
        next(before, None)
    for _ in before:
        pass
    left_in = [load(full.at[c, :, :, :, pl.ds(0, LEFT), :], left.at[0], left_sems.at[0])]
    right_in = [load(full.at[c, :, :, :, pl.ds(LEFT, RIGHT), :], right.at[0], right_sems.at[0])]
    left_in[0].wait()
    latent[...] = dot(wide(tok2, 0, D // TB), left[0].reshape(D, TB)).astype(BF)
    right_in[0].wait()
    back = jnp.zeros((2 * here, TB), F32)
    for j in range(CHUNKS):
        cots = wide(grad2, j * WIDE // TB, WIDE // TB)
        y, h = j // 2, slice((j % 2) * 2, (j % 2) * 2 + 2)
        back = back + dot(cots, right[0, y, h].reshape(WIDE, TB))
        q[y, h, :, LEFT : LEFT + RIGHT, :] = contract_rows(cots, latent[...]).astype(BF).reshape(2, 4, RIGHT, TB)
    next(sums[1])
    next(sums[2])
    back_c[...] = back.astype(BF)
    for j in range(4):
        product = contract_rows(wide(tok2, j * 8, 8), back_c[...])
        q[j, :, :, :LEFT, :] = product.astype(BF).reshape(4, 4, LEFT, TB)
    next(sums[0])
    to_sibling(mine, full.at[o], side_sems).wait()
    left_in.append(load(full.at[o, :, :, :, pl.ds(0, LEFT), :], left.at[1], left_sems.at[1]))
    right_in.append(load(full.at[o, :, :, :, pl.ds(LEFT, RIGHT), :], right.at[1], right_sems.at[1]))
    for n in range(16):
        load(full.at[:, n // 4, n % 4, :, pl.ds(LEFT + RIGHT, TB), :], tiles.at[:, pl.ds(4 * n, 4)], tile_sem)
    tiles_in = pltpu.make_async_copy(tiles, tiles, tile_sem)

    def running_sums(which, product, g0):
        def body(g, held):
            parts = [product(g * 8 + u) for u in range(8)]
            for u in range(8):
                t = g * 8 + u
                held = held * joins[which, 4, t] + parts[u]
                run[t] = held
            return held

        first = jnp.zeros((here, TB), F32) if g0 == 0 else run[g0 * 8 - 1]
        lax.fori_loop(g0, g0 + 16 // SLICES, body, first)

    def tile(which, t):
        return tiles[within(order[which, 1, t], 2), within(order[which, 2, t], 64)]

    def ahead(t):
        return dot(tok2[within(order[0, 0, t], D // TB), :here], tile(0, t))

    def behind(t):
        return contract_cols(grad2[within(order[1, 0, t], FF // TB), :here], tile(1, t))

    def work():
        left_in[1].wait()
        latent_o[...] = dot(wide(tok2, 0, D // TB, here), left[1].reshape(D, TB)).astype(BF)
        tiles_in.wait()
        run[EMPTY] = jnp.zeros((here, TB), F32)
        for n in range(SLICES):
            running_sums(0, ahead, n * 16 // SLICES)
            yield
        right_in[1].wait()
        back_o[...] = jnp.zeros((here, TB), F32)
        for j in range(CHUNKS):
            span = slice(j * WIDE, (j + 1) * WIDE)
            y, h = j // 2, slice((j % 2) * 2, (j % 2) * 2 + 2)
            rights = [right[k, y, h].reshape(WIDE, TB) for k in (0, 1)]
            back_o[...] += dot(wide(grad2, j * WIDE // TB, WIDE // TB, here), rights[1])
            dense = contract_cols(latent[:here], rights[0]) + contract_cols(latent_o[...], rights[1])
            for b in range(WIDE // TB):
                n = j * (WIDE // TB) + b
                out_v[:, n * TB : (n + 1) * TB] = (dense[:, b * TB : (b + 1) * TB] + run[within(order[0, 3, n], EMPTY + 1)]).astype(BF)
            pltpu.make_async_copy(out_v.at[:, span], out.at[:, span], out_sem).start()
            if j % 2:
                yield
        for n in range(SLICES):
            running_sums(1, behind, n * 16 // SLICES)
            yield
        back_h = back_o[...].astype(BF)
        for j in range(4):
            lefts = [left[k, j].reshape(1024, TB) for k in (0, 1)]
            dense = contract_cols(back_c[:here], lefts[0]) + contract_cols(back_h, lefts[1])
            for b in range(8):
                n = j * 8 + b
                back_v[:, n * TB : (n + 1) * TB] = (dense[:, b * TB : (b + 1) * TB] + run[within(order[1, 3, n], EMPTY + 1)]).astype(BF)
            if j % 2:
                yield
        pltpu.make_async_copy(back_v, back_out, back_sem).start()

    run_with(summing + [sums[0], sums[1], sums[2]], work())
    pltpu.make_async_copy(out_v, out, out_sem).wait()
    pltpu.make_async_copy(back_v, back_out, back_sem).wait()
    wire.finish()
    for swap in swaps:
        swap.wait_send()
    sums[4]()
    for k in (0, 1):
        half = slice(k * TB, (k + 1) * TB)
        left_grad[:, half] = total[k, :LEFT]
        right_grad[half, :] = total[k, LEFT : LEFT + 2 * TB].T[:, :RIGHT]
        tile_grad[k] = total[k, LEFT + RIGHT :]


def whole_step(rows, cols, left, right, tiles, tok, grad, scale):
    here = tok.shape[0]
    return pl.pallas_call(
        lambda *refs: kernel(scale, *refs),
        out_shape=(
            jax.ShapeDtypeStruct((here, FF), BF),
            jax.ShapeDtypeStruct((here, D), BF),
            jax.ShapeDtypeStruct((LEFT, R), F32),
            jax.ShapeDtypeStruct((R, RIGHT), F32),
            jax.ShapeDtypeStruct((2, TB, TB), F32),
            jax.ShapeDtypeStruct((2, SIDE, SIDE, SIDE, QROWS, TB), BF),
            jax.ShapeDtypeStruct(tok.shape, BF),
            jax.ShapeDtypeStruct(grad.shape, BF),
        ),
        in_specs=[pl.BlockSpec(memory_space=pltpu.SMEM)] * 2 + [VMEM] * 3 + [ANY] * 2,
        out_specs=(ANY,) * 2 + (VMEM,) * 3 + (ANY,) * 3,
        scratch_shapes=[
            pltpu.VMEM((SIDE, SIDE, SIDE, QROWS, TB), BF),
            pltpu.VMEM((2, SIDE, SIDE, SIDE, LEFT, TB), BF),
            pltpu.VMEM((2, SIDE, SIDE, SIDE, RIGHT, TB), BF),
            pltpu.VMEM((2, 64, TB, TB), BF),
            pltpu.VMEM((D // TB, 2 * here, TB), BF),
            pltpu.VMEM((FF // TB, 2 * here, TB), BF),
            pltpu.VMEM((EMPTY + 1, here, TB), F32),
            pltpu.VMEM((2 * here, TB), BF),
            pltpu.VMEM((here, TB), BF),
            pltpu.VMEM((2 * here, TB), BF),
            pltpu.VMEM((here, TB), F32),
            pltpu.VMEM((3, 2 * here, PIECE), BF),
            pltpu.VMEM((here, FF), BF),
            pltpu.VMEM((here, D), BF),
            pltpu.VMEM((SIDE, SIDE, SIDE, 16, TB), BF),
            pltpu.VMEM((3, 8, TB), jnp.int32),
            pltpu.VMEM((2, 8, TB), F32),
            pltpu.SMEM((3, 8, TB), jnp.int32),
            pltpu.SMEM((2, 8, TB), F32),
            pltpu.SemaphoreType.DMA((2,)),
            pltpu.SemaphoreType.DMA((2,)),
            pltpu.SemaphoreType.DMA,
            pltpu.SemaphoreType.DMA((2, 3)),
            pltpu.SemaphoreType.DMA((2,)),
            pltpu.SemaphoreType.DMA,
            pltpu.SemaphoreType.DMA,
            pltpu.SemaphoreType.DMA((120,)),
            pltpu.SemaphoreType.DMA((120,)),
            pltpu.SemaphoreType.DMA((2,)),
            pltpu.SemaphoreType.DMA((2,)),
            pltpu.SemaphoreType.DMA((2, 2)),
            pltpu.VMEM((QROWS, TB), BF),
            pltpu.VMEM((2, QROWS, TB), F32),
            pltpu.SemaphoreType.DMA((100,)),
            pltpu.SemaphoreType.DMA((100,)),
        ]
        + reduce_scratch(),
        compiler_params=pltpu.CompilerParams(
            collective_id=0, has_side_effects=True, vmem_limit_bytes=63 * 1024 * 1024
        ),
        name="whole_step",
    )(rows, cols, left, right, tiles, tok, grad)


def local(tokens, left_factor, right_factor, tile_values, tile_rows, tile_cols, grad_out):
    grad_scale = 1.0 / math.sqrt(tokens.shape[0] * lax.axis_size("fsdp") * lax.axis_size("rep"))
    return tuple(
        whole_step(tile_rows, tile_cols, left_factor, right_factor, tile_values, tokens, grad_out, grad_scale)[:5]
    )


def solution(mesh):
    placed = (
        P(("rep", "fsdp"), None),
        P("fsdp", None),
        P(None, "fsdp"),
        P("fsdp", None, None),
        P("fsdp"),
        P("fsdp"),
        P(("rep", "fsdp"), None),
    )
    return jax.shard_map(
        local,
        mesh=mesh,
        in_specs=placed,
        out_specs=(
            P(("rep", "fsdp"), None),
            P(("rep", "fsdp"), None),
            P("fsdp", None),
            P(None, "fsdp"),
            P("fsdp", None, None),
        ),
        check_vma=False,
    )
```

```python
import math

import jax
import jax.numpy as jnp
from jax import lax
from jax.experimental import pallas as pl
from jax.experimental.pallas import tpu as pltpu
from jax.sharding import PartitionSpec as P

D = 4096
FF = 14336
TB = 128
R = 256
SIDE = 4
LEFT = 64
RIGHT = 224
QROWS = LEFT + RIGHT + TB
MESH = pl.DeviceIdType.MESH
BF = jnp.bfloat16
F32 = jnp.float32
Y, H, X = 0, 1, 2
ANY = pl.BlockSpec(memory_space=pl.ANY)
VMEM = pl.BlockSpec(memory_space=pltpu.VMEM)


class Place:
    def __init__(self):
        rep, f = lax.axis_index("rep"), lax.axis_index("fsdp")
        self.l, self.c = rep // 2, rep % 2
        self.at = [f // 16, (f // 4) % 4, f % 4]
        self.s = 2 * self.l - 1
        self.sib = self.dev(core=1 - self.c)
        self.pair = self.dev(low=1 - self.l)
        self.out = self.dev(low=1 - self.l, step=(H, self.s))
        self.plus = {a: self.dev(step=(a, 1)) for a in (Y, X)}
        self.minus = {a: self.dev(step=(a, 3)) for a in (Y, X)}
        self.direct = {a: [self.dev(step=(a, k)) for k in (1, 3, 2)] for a in (Y, X)}
        self.direct[H] = [self.out, self.dev(step=(H, self.s)), self.dev(low=1 - self.l, step=(H, 2))]
        self.behind = self.dev(step=(H, -self.s))

    def dev(self, core=None, low=None, step=None):
        core = self.c if core is None else core
        low = self.l if low is None else low
        at = list(self.at)
        if step:
            at[step[0]] = (at[step[0]] + step[1] + 4) % 4
        return {"rep": low * 2 + core, "fsdp": (at[0] * 4 + at[1]) * 4 + at[2]}

    def greet(self):
        barrier = pltpu.get_barrier_semaphore()
        near = [self.sib, self.pair, self.behind] + [d for a in (Y, H, X) for d in self.direct[a]]
        for device in near:
            pl.semaphore_signal(barrier, inc=1, device_id=device, device_id_type=MESH)
        pl.semaphore_wait(barrier, len(near))


class Wire:
    def __init__(self, send_sems, recv_sems):
        self.send_sems, self.recv_sems = send_sems, recv_sems
        self.started = []

    def __call__(self, src, dst, device):
        k = len(self.started)
        copy = pltpu.make_async_remote_copy(
            src_ref=src,
            dst_ref=dst,
            send_sem=self.send_sems.at[k],
            recv_sem=self.recv_sems.at[k],
            device_id=device,
            device_id_type=MESH,
        )
        copy.start()
        self.started.append(copy)
        return copy

    def finish(self):
        for copy in self.started:
            copy.wait_send()


def view(ref, fixed, axis, j, row0, rows, half=None, chunk=None, chunks=1):
    sel = list(fixed)
    sel[axis] = j
    r0, n = row0, rows
    free = [a for a in range(3) if a != axis and fixed[a] is None]
    if half is not None:
        if free:
            width = 2 // chunks
            start = half * 2 + (0 if chunk is None else chunk * width)
            sel[free[0]] = pl.ds(start, width if chunk is not None else 2)
        elif rows % 32 == 0:
            n = rows // 2
            r0 = row0 + half * n
        else:
            cut = (rows // 32 + 1) * 16
            r0, n = (row0, cut) if half == 0 else (row0 + cut, rows - cut)
    sel = [slice(None) if v is None else v for v in sel]
    return ref.at[sel[0], sel[1], sel[2], pl.ds(r0, n), :]


GATHER = (((X, Y, H), 0, 128), ((Y, H, X), 128, 160), ((H, X, Y), 288, 128))


def spread(me, axis, send, got, ready):
    i = me.at[axis]
    across = (i + 2) % 4
    if axis == H:
        l, s = me.l, me.s
        up, down = (i + s + 4) % 4, (i - s + 4) % 4
        a, b = send(i, 1 - l, me.out), send(i, l, me.out)
        yield
        a.wait_recv()
        f = send(up, l, me.pair)
        got(up, l)
        yield
        b.wait_recv()
        e = send(up, 1 - l, me.pair)
        got(up, 1 - l)
        ready(up)
        yield
        f.wait_recv()
        g = send(down, 1 - l, me.out)
        got(down, 1 - l)
        yield
        e.wait_recv()
        got(down, l)
        ready(down)
        yield
        g.wait_recv()
        w = send(across, l, me.pair)
        got(across, l)
        yield
        w.wait_recv()
        got(across, 1 - l)
        ready(across)
    else:
        plus, minus = me.plus[axis], me.minus[axis]
        after, before = (i + 1) % 4, (i + 3) % 4
        a0, b1 = send(i, 0, plus), send(i, 1, minus)
        a1, b0 = send(i, 1, plus), send(i, 0, minus)
        yield
        a0.wait_recv()
        c0 = send(before, 0, plus)
        got(before, 0)
        b1.wait_recv()
        c1 = send(after, 1, minus)
        got(after, 1)
        yield
        a1.wait_recv()
        got(before, 1)
        ready(before)
        b0.wait_recv()
        got(after, 0)
        ready(after)
        yield
        c0.wait_recv()
        got(across, 0)
        c1.wait_recv()
        got(across, 1)
        ready(across)


REDUCE = (((H, Y, X), 0, 96), ((X, H, Y), 96, 96), ((Y, X, H), 192, 96), ((Y, X, H), 288, 128))


def add_into(dst, *terms):
    shape = dst.shape
    lead = shape[:-2]
    rows = shape[-2]
    count = math.prod(lead)

    def body(k, _):
        at = []
        for n in reversed(lead):
            at.append(k % n)
            k = k // n
        at = tuple(reversed(at))
        for r in range(0, rows, 16):
            here = at + (pl.ds(r, 16), slice(None))
            total = terms[0][here].astype(F32)
            for term in terms[1:]:
                total = total + term[here].astype(F32)
            dst[here] = total.astype(dst.dtype)
        return 0

    if count == 1:
        body(0, 0)
    else:
        lax.fori_loop(0, count, body, 0)


def reduce_parts(me, scale, q_ref, out, scratch):
    (send_sems, recv_sems), scratch = scratch[:2], scratch[2:]
    wire = Wire(send_sems, recv_sems)
    per_part = len(scratch) // len(REDUCE)

    def part(n):
        order, row0, rows = REDUCE[n]
        pool = list(scratch[n * per_part : (n + 1) * per_part])
        held = q_ref
        for stage, axis in enumerate(order):
            fixed = [me.at[a] if a in order[:stage] else None for a in range(3)]
            if stage:
                fixed = [0 if a in order[:stage] else None for a in range(3)]
            base = row0 if stage == 0 else 0
            staged = held
            nxt = pool.pop(0)
            first, second, third = pool.pop(0), pool.pop(0), pool.pop(0)
            dims = [a for a in range(3) if a != axis and fixed[a] is None]
            i = me.at[axis]

            def blk(ref, j, half=None, chunk=None, chunks=1):
                at0 = base if ref is held or ref is staged else 0
                return view(ref, fixed, axis, j, at0, rows, half, chunk, chunks)

            def send(j, half, dst, dst_j, device, extra=None, chunk=None, chunks=1):
                src = blk(staged, j, half, chunk, chunks)
                if extra is not None:
                    add_into(src, blk(held, j, half, chunk, chunks), extra)
                return wire(src, blk(dst, dst_j, half, chunk, chunks), device)

            if axis == H:
                l, s = me.l, me.s
                up, down, across = (i + s + 4) % 4, (i - s + 4) % 4, (i + 2) % 4
                chunks = 2 if stage == 0 else 1
                ids = range(chunks) if stage == 0 else (None,)
                a = [send(across, l, first, 0, me.pair, None, q, chunks) for q in ids]
                b = [send(down, 1 - l, second, 0, me.pair, None, q, chunks) for q in ids]
                yield
                c = []
                for k, q in enumerate(ids):
                    a[k].wait_recv()
                    c.append(send(across, 1 - l, first, 1, me.out, blk(first, 0, 1 - l, q, chunks), q, chunks))
                yield
                d = []
                for k, q in enumerate(ids):
                    b[k].wait_recv()
                    d.append(send(up, l, third, 0, me.out, blk(second, 0, l, q, chunks), q, chunks))
                yield
                e = []
                for k, q in enumerate(ids):
                    c[k].wait_recv()
                    e.append(send(down, l, second, 0, me.pair, blk(first, 1, l, q, chunks), q, chunks))
                yield
                f = []
                for k, q in enumerate(ids):
                    e[k].wait_recv()
                    f.append(send(up, 1 - l, third, 0, me.out, blk(second, 0, 1 - l, q, chunks), q, chunks))
                yield
                for k, q in enumerate(ids):
                    d[k].wait_recv()
                    add_into(blk(nxt, 0, 1 - l, q, chunks), blk(held, i, 1 - l, q, chunks), blk(third, 0, 1 - l, q, chunks))
                yield
                for k, q in enumerate(ids):
                    f[k].wait_recv()
                    add_into(blk(nxt, 0, l, q, chunks), blk(held, i, l, q, chunks), blk(third, 0, l, q, chunks))
            else:
                plus, minus = me.plus[axis], me.minus[axis]
                after, before, across = (i + 1) % 4, (i + 3) % 4, (i + 2) % 4
                a0 = send(across, 0, first, 0, plus)
                a1 = send(across, 1, first, 0, minus)
                b1 = send(after, 1, second, 0, plus)
                b0 = send(before, 0, third, 0, minus)
                yield
                a0.wait_recv()
                c0 = send(after, 0, second, 0, plus, blk(first, 0, 0))
                a1.wait_recv()
                c1 = send(before, 1, third, 0, minus, blk(first, 0, 1))
                yield
                b1.wait_recv()
                b0.wait_recv()
                yield
                c0.wait_recv()
                c1.wait_recv()
                for half in (0, 1):
                    add_into(blk(nxt, 0, half), blk(held, i, half), blk(second, 0, half), blk(third, 0, half))
            held = nxt
            yield
        other = pool.pop(0)
        swap = wire(held, other, me.pair)
        yield
        swap.wait_recv()
        place = out.at[me.c, pl.ds(row0, rows), :]
        place[...] = (held[0, 0, 0] + other[0, 0, 0]) * scale
        final = wire(place, place, me.sib)
        yield
        final.wait_recv()

    return [part(n) for n in range(len(REDUCE))] + [wire.finish]


def run_with(active, work):
    while active:
        for run in list(active):
            try:
                next(run)
            except StopIteration:
                active.remove(run)
        next(work, None)
    for _ in work:
        pass


def reduce_scratch():
    shapes = []
    for order, _, rows in REDUCE:
        dims = [SIDE] * 3
        for stage, axis in enumerate(order):
            wire = BF if stage < 1 else F32
            dims[axis] = 1
            shapes.append(pltpu.VMEM(tuple(dims) + (rows, TB), F32))
            two = list(dims)
            two[axis] = 2
            shapes.append(pltpu.VMEM(tuple(two if axis == H else dims) + (rows, TB), wire))
            shapes += [pltpu.VMEM(tuple(dims) + (rows, TB), wire)] * 2
        shapes.append(pltpu.VMEM((1, 1, 1, rows, TB), F32))
    return shapes


CHUNKS = 8
PER = 64 // CHUNKS
WIDE = PER * RIGHT
SLICES = 2
EMPTY = 128
PIECE = 2048


def contract_rows(left, right):
    return lax.dot_general(left, right, (((0,), (0,)), ((), ())), preferred_element_type=F32)


def contract_cols(left, right):
    return lax.dot_general(left, right, (((1,), (1,)), ((), ())), preferred_element_type=F32)


def dot(left, right):
    return jnp.dot(left, right, preferred_element_type=F32)


def wide(ref, first, count, rows=None):
    return jnp.concatenate([ref[n] if rows is None else ref[n, :rows] for n in range(first, first + count)], 1)


def load(src, dst, sem):
    copy = pltpu.make_async_copy(src, dst, sem)
    copy.start()
    return copy


def within(index, count):
    return jnp.minimum(jnp.maximum(index, 0), count - 1)


def sort_tiles(marks, order, joins):
    held = marks[...].reshape(64 * 16, TB)
    i0 = lax.broadcasted_iota(jnp.int32, (128, 1024), 0)
    i1 = lax.broadcasted_iota(jnp.int32, (128, 1024), 1)
    columns, rows = [], []
    for base in (0, 8):
        pick = (i1 == (i0 >> 1) * 16 + (i0 & 1) * 4 + base).astype(F32).astype(BF)
        columns.append(dot(pick, held))
        rows.append(lax.dot_general(held, pick, (((0,), (1,)), ((), ())), preferred_element_type=F32))
    t0 = lax.broadcasted_iota(jnp.int32, (128, 128), 0).astype(F32)
    t1 = lax.broadcasted_iota(jnp.int32, (128, 128), 1).astype(F32)
    s8 = lax.broadcasted_iota(jnp.int32, (8, 128), 0)
    lane = lax.broadcasted_iota(jnp.int32, (8, 128), 1)
    one = lambda truth: jnp.where(truth, 1.0, 0.0)
    for which, key in ((0, 1), (1, 0)):
        by0, by1, other = columns[key], rows[key], rows[1 - key]
        rank = jnp.sum(one(by1 * 128 + t1 < by0 * 128 + t0), 1, keepdims=True)
        moved = one(rank == t1).astype(BF)
        earlier = jnp.max(one(by0 == by1) * one(t0 < t1), 0, keepdims=True)
        upto = jnp.sum(one(by0 <= t1), 0, keepdims=True)
        present = jnp.max(one(by0 == t1), 0, keepdims=True)
        slot = jnp.where(present > 0.5, upto - 1, float(EMPTY))
        value = jnp.where(s8 == 0, other[:8], 0.0)
        value = jnp.where(s8 == 1, (lane & 1).astype(F32), value)
        value = jnp.where(s8 == 2, (lane >> 1).astype(F32), value)
        value = jnp.where(s8 == 4, jnp.broadcast_to(earlier, (8, 128)), value)
        found = dot(value.astype(BF), moved)
        found = jnp.where(s8 == 3, jnp.broadcast_to(slot, (8, 128)), found)
        order[which] = found.astype(jnp.int32)
        joins[which] = found
    order[2] = jnp.where(s8 == 0, rows[0][:8], rows[1][:8]).astype(jnp.int32)


def kernel(scale, tile_rows, tile_cols, left_own, right_own, tiles_own, tok, grad, out, back_out, left_grad, right_grad, tile_grad, full, tok_s, grad_s, *scratch):
    (q, left, right, tiles, tok2, grad2, run, latent, latent_o, back_c, back_o, stage, out_v, back_v) = scratch[:14]
    (marks, order_v, joins_v, order, joins) = scratch[14:19]
    left_sems, right_sems, tile_sem, stage_sems, order_sems, out_sem, back_sem = scratch[19:26]
    send_sems, recv_sems, local_sems, side_sems, wide_sems = scratch[26:31]
    me = Place()
    c, o = me.c, 1 - me.c
    here = tok.shape[0]
    mine = full.at[c]
    at = me.at
    pay, total = scratch[31:33]
    pay[:LEFT] = jnp.where(c == 0, left_own[:, :TB], left_own[:, TB:])
    turned = right_own[pl.ds(pl.multiple_of(c * TB, TB), TB), :].astype(F32)
    turned = jnp.concatenate([turned, jnp.zeros((TB, 2 * TB - RIGHT), F32)], 1).T
    pay[LEFT : LEFT + RIGHT] = turned[:RIGHT].astype(BF)
    pay[LEFT + RIGHT :] = tiles_own[c]
    found = [ref[k].astype(F32) for ref in (tile_rows, tile_cols) for k in (0, 1)]
    group = lax.broadcasted_iota(jnp.int32, (16, TB), 0) // 4
    mark = jnp.full((16, TB), found[3], F32)
    for k in (2, 1, 0):
        mark = jnp.where(group == k, found[k], mark)
    marks[at[0], at[1], at[2]] = mark.astype(BF)
    own = load(pay, mine.at[at[0], at[1], at[2]], local_sems.at[0])
    me.greet()
    own.wait()
    wire = Wire(send_sems, recv_sems)
    active = []
    known = set()

    def to_sibling(src, dst, pair):
        return pltpu.make_async_remote_copy(
            src_ref=src,
            dst_ref=dst,
            send_sem=pair.at[0],
            recv_sem=pair.at[1],
            device_id=me.sib,
            device_id_type=MESH,
        )

    def positions():
        for seg, axis in (
            (marks.at[at[0], at[1], at[2]], H),
            (marks.at[at[0], :, at[2]], X),
            (marks.at[at[0]], Y),
        ):
            copies = [wire(seg, seg, device) for device in me.direct[axis]]
            yield
            for copy in copies:
                copy.wait_recv()
        known.add("marks")

    def part(order3, row0, rows):
        one, two, three = order3

        def piece(sel, half=None):
            sel = [sel.get(a, slice(None)) for a in range(3)]
            if half is not None:
                sel[one] = pl.ds(half * 2, 2)
            return mine.at[sel[0], sel[1], sel[2], pl.ds(row0, rows), :]

        def last(j2):
            def send(j, half, device):
                ref = piece({two: j2, three: j}, half)
                return wire(ref, ref, device)

            def got(j, half):
                ref = piece({two: j2, three: j}, half)
                to_sibling(ref, ref, side_sems).start()

            ref = piece({two: j2, three: at[three]})
            to_sibling(ref, ref, side_sems).start()
            return spread(me, three, send, got, lambda j: None)

        def start_last(j2):
            nonlocal_run = last(j2)
            next(nonlocal_run)
            active.append(nonlocal_run)

        def send(j, half, device):
            ref = piece({two: j, three: at[three]}, half)
            return wire(ref, ref, device)

        seed = piece({a: at[a] for a in range(3)})
        seeds = [wire(seed, seed, device) for device in me.direct[one]]
        yield
        for copy in seeds:
            copy.wait_recv()
        spreading = spread(me, two, send, lambda j, half: None, start_last)
        next(spreading)
        start_last(at[two])
        active.append(spreading)

    active.append(positions())
    for p in GATHER:
        active.append(part(*p))
    for each in active:
        next(each)
    swaps = [to_sibling(tok, tok_s, wide_sems.at[0]), to_sibling(grad, grad_s, wide_sems.at[1])]
    for swap in swaps:
        swap.start()
    sums = reduce_parts(me, scale, q, total, scratch[33:])
    pieces = [(tok, tok_s, tok2, n) for n in range(D // PIECE)] + [(grad, grad_s, grad2, n) for n in range(FF // PIECE)]

    def fetch(k):
        first, second, _, n = pieces[k]
        span = pl.ds(n * PIECE, PIECE)
        return [
            load(first.at[:, span], stage.at[k % 3, pl.ds(0, here)], stage_sems.at[0, k % 3]),
            load(second.at[:, span], stage.at[k % 3, pl.ds(here, here)], stage_sems.at[1, k % 3]),
        ]

    def tile_part(g, _):
        for u in range(8):
            t = 2 * (g * 8 + u) + c
            product = contract_rows(tok2[within(order[2, 0, t], D // TB)], grad2[within(order[2, 1, t], FF // TB)])
            q[g // 2, (g % 2) * 2 + u // 4, u % 4, LEFT + RIGHT :, :] = product.astype(BF)
        return 0

    def early():
        yield
        yield
        for swap in swaps:
            swap.wait_recv()
        coming = [fetch(k) for k in range(3)]
        for k, (_, _, held, n) in enumerate(pieces):
            for copy in coming[k]:
                copy.wait()
            for b in range(PIECE // TB):
                held[n * (PIECE // TB) + b] = stage[k % 3, :, b * TB : (b + 1) * TB]
            if k + 3 < len(pieces):
                coming.append(fetch(k + 3))
            if k % 3 == 2:
                yield
        while "marks" not in known:
            yield
        sort_tiles(marks, order_v, joins_v)
        filed = [load(order_v, order, order_sems.at[0]), load(joins_v, joins, order_sems.at[1])]
        for copy in filed:
            copy.wait()
        yield
        for n in range(2):
            lax.fori_loop(n * 4, n * 4 + 4, tile_part, 0)
            yield
        next(sums[3])
        summing.append(sums[3])

    summing = []
    before = early()
    while active:
        for each in list(active) + list(summing):
            if next(each, "end") == "end":
                (active if each in active else summing).remove(each)
        next(before, None)
    for _ in before:
        pass
    left_in = [load(full.at[c, :, :, :, pl.ds(0, LEFT), :], left.at[0], left_sems.at[0])]
    right_in = [load(full.at[c, :, :, :, pl.ds(LEFT, RIGHT), :], right.at[0], right_sems.at[0])]
    left_in[0].wait()
    latent[...] = dot(wide(tok2, 0, D // TB), left[0].reshape(D, TB)).astype(BF)
    right_in[0].wait()
    back = jnp.zeros((2 * here, TB), F32)
    for j in range(CHUNKS):
        cots = wide(grad2, j * WIDE // TB, WIDE // TB)
        y, h = j // 2, slice((j % 2) * 2, (j % 2) * 2 + 2)
        back = back + dot(cots, right[0, y, h].reshape(WIDE, TB))
        q[y, h, :, LEFT : LEFT + RIGHT, :] = contract_rows(cots, latent[...]).astype(BF).reshape(2, 4, RIGHT, TB)
    next(sums[1])
    next(sums[2])
    back_c[...] = back.astype(BF)
    for j in range(4):
        product = contract_rows(wide(tok2, j * 8, 8), back_c[...])
        q[j, :, :, :LEFT, :] = product.astype(BF).reshape(4, 4, LEFT, TB)
    next(sums[0])
    to_sibling(mine, full.at[o], side_sems).wait()
    left_in.append(load(full.at[o, :, :, :, pl.ds(0, LEFT), :], left.at[1], left_sems.at[1]))
    right_in.append(load(full.at[o, :, :, :, pl.ds(LEFT, RIGHT), :], right.at[1], right_sems.at[1]))
    for n in range(16):
        load(full.at[:, n // 4, n % 4, :, pl.ds(LEFT + RIGHT, TB), :], tiles.at[:, pl.ds(4 * n, 4)], tile_sem)
    tiles_in = pltpu.make_async_copy(tiles, tiles, tile_sem)

    def running_sums(which, product, g0):
        def body(g, held):
            parts = [product(g * 8 + u) for u in range(8)]
            for u in range(8):
                t = g * 8 + u
                held = held * joins[which, 4, t] + parts[u]
                run[t] = held
            return held

        first = jnp.zeros((here, TB), F32) if g0 == 0 else run[g0 * 8 - 1]
        lax.fori_loop(g0, g0 + 16 // SLICES, body, first)

    def tile(which, t):
        return tiles[within(order[which, 1, t], 2), within(order[which, 2, t], 64)]

    def ahead(t):
        return dot(tok2[within(order[0, 0, t], D // TB), :here], tile(0, t))

    def behind(t):
        return contract_cols(grad2[within(order[1, 0, t], FF // TB), :here], tile(1, t))

    def work():
        left_in[1].wait()
        latent_o[...] = dot(wide(tok2, 0, D // TB, here), left[1].reshape(D, TB)).astype(BF)
        tiles_in.wait()
        run[EMPTY] = jnp.zeros((here, TB), F32)
        for n in range(SLICES):
            running_sums(0, ahead, n * 16 // SLICES)
            yield
        right_in[1].wait()
        back_o[...] = jnp.zeros((here, TB), F32)
        for j in range(CHUNKS):
            span = slice(j * WIDE, (j + 1) * WIDE)
            y, h = j // 2, slice((j % 2) * 2, (j % 2) * 2 + 2)
            rights = [right[k, y, h].reshape(WIDE, TB) for k in (0, 1)]
            back_o[...] += dot(wide(grad2, j * WIDE // TB, WIDE // TB, here), rights[1])
            dense = contract_cols(latent[:here], rights[0]) + contract_cols(latent_o[...], rights[1])
            for b in range(WIDE // TB):
                n = j * (WIDE // TB) + b
                out_v[:, n * TB : (n + 1) * TB] = (dense[:, b * TB : (b + 1) * TB] + run[within(order[0, 3, n], EMPTY + 1)]).astype(BF)
            pltpu.make_async_copy(out_v.at[:, span], out.at[:, span], out_sem).start()
            if j % 2:
                yield
        for n in range(SLICES):
            running_sums(1, behind, n * 16 // SLICES)
            yield
        back_h = back_o[...].astype(BF)
        for j in range(4):
            lefts = [left[k, j].reshape(1024, TB) for k in (0, 1)]
            dense = contract_cols(back_c[:here], lefts[0]) + contract_cols(back_h, lefts[1])
            for b in range(8):
                n = j * 8 + b
                back_v[:, n * TB : (n + 1) * TB] = (dense[:, b * TB : (b + 1) * TB] + run[within(order[1, 3, n], EMPTY + 1)]).astype(BF)
            if j % 2:
                yield
        pltpu.make_async_copy(back_v, back_out, back_sem).start()

    run_with(summing + [sums[0], sums[1], sums[2]], work())
    pltpu.make_async_copy(out_v, out, out_sem).wait()
    pltpu.make_async_copy(back_v, back_out, back_sem).wait()
    wire.finish()
    for swap in swaps:
        swap.wait_send()
    sums[4]()
    for k in (0, 1):
        half = slice(k * TB, (k + 1) * TB)
        left_grad[:, half] = total[k, :LEFT]
        right_grad[half, :] = total[k, LEFT : LEFT + 2 * TB].T[:, :RIGHT]
        tile_grad[k] = total[k, LEFT + RIGHT :]


def whole_step(rows, cols, left, right, tiles, tok, grad, scale):
    here = tok.shape[0]
    return pl.pallas_call(
        lambda *refs: kernel(scale, *refs),
        out_shape=(
            jax.ShapeDtypeStruct((here, FF), BF),
            jax.ShapeDtypeStruct((here, D), BF),
            jax.ShapeDtypeStruct((LEFT, R), F32),
            jax.ShapeDtypeStruct((R, RIGHT), F32),
            jax.ShapeDtypeStruct((2, TB, TB), F32),
            jax.ShapeDtypeStruct((2, SIDE, SIDE, SIDE, QROWS, TB), BF),
            jax.ShapeDtypeStruct(tok.shape, BF),
            jax.ShapeDtypeStruct(grad.shape, BF),
        ),
        in_specs=[pl.BlockSpec(memory_space=pltpu.SMEM)] * 2 + [VMEM] * 3 + [ANY] * 2,
        out_specs=(ANY,) * 2 + (VMEM,) * 3 + (ANY,) * 3,
        scratch_shapes=[
            pltpu.VMEM((SIDE, SIDE, SIDE, QROWS, TB), BF),
            pltpu.VMEM((2, SIDE, SIDE, SIDE, LEFT, TB), BF),
            pltpu.VMEM((2, SIDE, SIDE, SIDE, RIGHT, TB), BF),
            pltpu.VMEM((2, 64, TB, TB), BF),
            pltpu.VMEM((D // TB, 2 * here, TB), BF),
            pltpu.VMEM((FF // TB, 2 * here, TB), BF),
            pltpu.VMEM((EMPTY + 1, here, TB), F32),
            pltpu.VMEM((2 * here, TB), BF),
            pltpu.VMEM((here, TB), BF),
            pltpu.VMEM((2 * here, TB), BF),
            pltpu.VMEM((here, TB), F32),
            pltpu.VMEM((3, 2 * here, PIECE), BF),
            pltpu.VMEM((here, FF), BF),
            pltpu.VMEM((here, D), BF),
            pltpu.VMEM((SIDE, SIDE, SIDE, 16, TB), BF),
            pltpu.VMEM((3, 8, TB), jnp.int32),
            pltpu.VMEM((2, 8, TB), F32),
            pltpu.SMEM((3, 8, TB), jnp.int32),
            pltpu.SMEM((2, 8, TB), F32),
            pltpu.SemaphoreType.DMA((2,)),
            pltpu.SemaphoreType.DMA((2,)),
            pltpu.SemaphoreType.DMA,
            pltpu.SemaphoreType.DMA((2, 3)),
            pltpu.SemaphoreType.DMA((2,)),
            pltpu.SemaphoreType.DMA,
            pltpu.SemaphoreType.DMA,
            pltpu.SemaphoreType.DMA((120,)),
            pltpu.SemaphoreType.DMA((120,)),
            pltpu.SemaphoreType.DMA((2,)),
            pltpu.SemaphoreType.DMA((2,)),
            pltpu.SemaphoreType.DMA((2, 2)),
            pltpu.VMEM((QROWS, TB), BF),
            pltpu.VMEM((2, QROWS, TB), F32),
            pltpu.SemaphoreType.DMA((100,)),
            pltpu.SemaphoreType.DMA((100,)),
        ]
        + reduce_scratch(),
        compiler_params=pltpu.CompilerParams(
            collective_id=0, has_side_effects=True, vmem_limit_bytes=63 * 1024 * 1024
        ),
        name="whole_step",
    )(rows, cols, left, right, tiles, tok, grad)


def local(tokens, left_factor, right_factor, tile_values, tile_rows, tile_cols, grad_out):
    grad_scale = 1.0 / math.sqrt(tokens.shape[0] * lax.axis_size("fsdp") * lax.axis_size("rep"))
    return tuple(
        whole_step(tile_rows, tile_cols, left_factor, right_factor, tile_values, tokens, grad_out, grad_scale)[:5]
    )


def solution(mesh):
    placed = (
        P(("rep", "fsdp"), None),
        P("fsdp", None),
        P(None, "fsdp"),
        P("fsdp", None, None),
        P("fsdp"),
        P("fsdp"),
        P(("rep", "fsdp"), None),
    )
    return jax.shard_map(
        local,
        mesh=mesh,
        in_specs=placed,
        out_specs=(
            P(("rep", "fsdp"), None),
            P(("rep", "fsdp"), None),
            P("fsdp", None),
            P(None, "fsdp"),
            P("fsdp", None, None),
        ),
        check_vma=False,
    )
```
